32 devices in a mesh: tm: 16 (over z, x, core), tok: 2 (over y).
Axes of the slice: x: 2, y: 2, z: 4, core: 2. Of those that a mesh axis runs over, the one named last changes fastest.
Arguments:
- queries: bfloat16 [32, 256, 1024], P('tm', 'tok'), may hold values from -6 to 6
- keys: bfloat16 [32, 256, 1024], P('tm', 'tok'), may hold values from -6 to 6
- values: bfloat16 [32, 256, 1024], P('tm', 'tok'), may hold values from -6 to 6
- epi_dev: int32 [32, 6], replicated, may hold values from 0 to 15, all different within a row; in each aligned block of 2 rows (0 to 1, 2 to 3, ...) at most 2 rows name the same one
- epi_frame: int32 [32, 6], replicated, may hold values from 0 to 1
- epi_block: int32 [32, 6], replicated, may hold values from 0 to 1
- valid: int32 [32, 6], replicated, may hold values 0 or 1
- ref_local: int32 [4], replicated, may hold values from 0 to 7
Outputs:
- attended: bfloat16 [32, 256, 1024], P('tm', 'tok')
The draws below stay inside these ranges and needn't reach their ends.
Inputs may be any that keep to these rules, and one draw needn't show every extreme that they name: `epi_dev`: the 6 values of one frame differ. Among the frames of one index of tm (aligned blocks of 2 frames), no value is named by more than 2 entries, a bound that some block reaches.
All inputs are finite; a program needn't handle non-finite values.
Results may differ from the reference program's by a relative error of at most 0.0032.
Values may be sent and summed in bfloat16 or wider, within the bound.
No kernel may reach another device: no remote copies, remote signals or barrier semaphores. Data moves between devices by JAX's collectives and lax.ppermute only.
A program may use at most 128 MiB of HBM per device.

```python
import math
import jax
import jax.numpy as jnp
import numpy as np
from jax import lax

HEADS = 16
HEAD_DIM = 64
BLOCK = 128
FRAMES_DEV = 2
ENTRIES = 6
CAPACITY = 2
SPAN = 4
WIDTH = 1024
FRAMES = 32
TOKENS = 256
GROUPS = 4
N_TM = 16
N_TOK = 2


def drawn_pair(key):
    key_q, key_k = jax.random.split(jax.random.fold_in(key, 4242), 2)
    full_shape = (FRAMES, TOKENS, WIDTH)
    query_table = jnp.clip(1.6 * jax.random.normal(key_q, full_shape, jnp.float32), -6.0, 6.0)
    key_table = jnp.clip(1.6 * jax.random.normal(key_k, full_shape, jnp.float32), -6.0, 6.0)
    return (query_table, key_table)


def draw_queries(key, part):
    return drawn_pair(key)[0].astype(jnp.bfloat16)


def draw_keys(key, part):
    return drawn_pair(key)[1].astype(jnp.bfloat16)


def touch_ends(entries, stream_key, low, top_value):
    index_at = [jax.random.randint(jax.random.fold_in(stream_key, axis), (), 0, length) for axis, length in enumerate(entries.shape)]
    widest = entries.shape.index(max(entries.shape))
    neighbour = index_at[:widest] + [(index_at[widest] + 1) % entries.shape[widest]] + index_at[widest + 1:]
    return entries.at[tuple(index_at)].set(low).at[tuple(neighbour)].set(top_value)


def block_levels(key, dims, cuts, least, largest):
    def one(position, parts):
        heights = jax.random.uniform(jax.random.fold_in(jax.random.fold_in(key, 6), position), (parts,), jnp.float32, least / len(cuts), largest / len(cuts))
        return jnp.repeat(jnp.exp(heights), dims[position] // parts).reshape((-1,) + (1,) * (len(dims) - position - 1))

    factor_of = one(*cuts[0])
    for cut in cuts[1:]:
        factor_of = factor_of * one(*cut)
    return factor_of


def deal_out(own_key, own, number, rows, count, top, most, skew):
    ranking = jax.random.permutation(own_key, count)
    packed, ordinary = load_shares(count, rows * top, most, skew, True), load_shares(count, rows * top, most, skew, False)
    places = jnp.arange(count)

    def named(tallies, turn):
        used = int((tallies > 0).sum())
        fixed = max(1, used // 4)
        moved = fixed + (places - fixed + turn * (used - fixed)) % max(1, count - fixed)
        return jnp.zeros((count,), jnp.int32).at[ranking[jnp.where(places < fixed, places, moved)]].set(jnp.asarray(tallies, jnp.int32))

    tallies = jnp.where(number % 4 == 0, named(packed, number // 4), named(ordinary, number - number // 4 - 1))
    mixed = jax.random.permutation(jax.random.fold_in(own, 3), count)
    donor, receiver = mixed[0:count // 2 * 2:2], mixed[1:count // 2 * 2:2]
    room = jnp.minimum(tallies[donor] - 1, most - tallies[receiver]) // 2
    room = jnp.where((donor == ranking[0]) | (receiver == ranking[0]) | (tallies[receiver] == 0), 0, jnp.maximum(room, 0))
    moved = jax.random.randint(jax.random.fold_in(own, 4), (count // 2,), 0, 1 << 20) % (room + 1)
    tallies = tallies.at[donor].add(-moved).at[receiver].add(moved)
    labels = jnp.searchsorted(jnp.cumsum(tallies), jnp.arange(rows * top), side="right").astype(jnp.int32)
    listing = labels.reshape(top, rows).T
    listing = listing[jax.random.permutation(jax.random.fold_in(own, 1), rows)]
    turn = jax.random.randint(jax.random.fold_in(own, 2), (rows, 1), 0, top)
    return jnp.take_along_axis(listing, (jnp.arange(top)[None, :] + turn) % top, axis=1)


def load_shares(amount, total, most, slope, full):
    portions = [(1 << 20) // math.isqrt(rank ** slope) + 1 for rank in range(1, amount + 1)]
    largest = most if full else min(most, max(-(-total // amount), total * portions[0] // sum(portions)))
    least = 1 if total - largest >= amount - 1 else 0
    given, spare = [largest] + [least] * (amount - 1), total - largest - least * (amount - 1)
    while spare > 0:
        free = [i for i in range(1, amount) if given[i] < largest] or [i for i in range(1, amount) if given[i] < most]
        whole, remaining = sum([portions[i] for i in free]), spare
        for i in free:
            more = min(most - given[i], max(1, remaining * portions[i] // whole), spare)
            given[i] = given[i] + more
            spare = spare - more
    return np.array(given)


def bell_draw(rng, dims, spread, most, shards=(), kind=jnp.bfloat16):
    values = jax.random.normal(rng, dims, jnp.float32) * spread
    if len(shards) > 0:
        values = block_levels(rng, dims, shards, -0.22, 0.18) * values
    return jnp.clip(values, min=-most, max=most).astype(kind)


def setup_inputs(seed: int = 0) -> dict:
    key_of = jax.random.split(jax.random.key(seed), 9)
    queries = draw_queries(jax.random.fold_in(key_of[8], 71), 0)
    keys = draw_keys(jax.random.fold_in(key_of[8], 71), 0)
    values = bell_draw(key_of[2], (FRAMES, TOKENS, WIDTH), 1.0, 6.0, ((0, 16), (1, 2)))
    epi_dev_keys = jax.random.split(jax.random.fold_in(key_of[3], 1), FRAMES // FRAMES_DEV)
    epi_dev_turns = jax.random.permutation(jax.random.fold_in(key_of[3], 3), FRAMES // FRAMES_DEV)
    epi_dev = jax.vmap(lambda own, number: deal_out(jax.random.fold_in(key_of[3], 2), own, number, FRAMES_DEV, N_TM, ENTRIES, CAPACITY, 2))(epi_dev_keys, epi_dev_turns).reshape((FRAMES, ENTRIES))
    epi_frame = touch_ends(jax.random.randint(key_of[4], (FRAMES, ENTRIES), 0, FRAMES_DEV), jax.random.fold_in(key_of[4], 1), 0, FRAMES_DEV - 1).astype(jnp.int32)
    epi_block = touch_ends(jax.random.randint(key_of[5], (FRAMES, ENTRIES), 0, N_TOK), jax.random.fold_in(key_of[5], 1), 0, N_TOK - 1).astype(jnp.int32)
    valid = touch_ends((jax.random.randint(key_of[6], (FRAMES, ENTRIES), 0, 4) < 3).astype(jnp.int32), jax.random.fold_in(key_of[6], 1), 0, 1)
    ref_local = touch_ends(jax.random.randint(key_of[7], (GROUPS,), 0, SPAN * FRAMES_DEV), jax.random.fold_in(key_of[7], 1), 0, (SPAN * FRAMES_DEV) - 1).astype(jnp.int32)
    return dict(queries=queries, keys=keys, values=values, epi_dev=epi_dev, epi_frame=epi_frame, epi_block=epi_block, valid=valid, ref_local=ref_local)


def reference(queries, keys, values, epi_dev, epi_frame, epi_block, valid, ref_local):
    head_q = queries.reshape(FRAMES, TOKENS, HEADS, HEAD_DIM)
    head_k = keys.reshape(FRAMES, TOKENS, HEADS, HEAD_DIM)
    head_v = values.reshape(FRAMES, TOKENS, HEADS, HEAD_DIM)
    source = (epi_dev * FRAMES_DEV + epi_frame).astype(jnp.int32)
    group_frames = SPAN * FRAMES_DEV
    score_scale = HEAD_DIM ** -0.5
    block_rows = math.gcd(TOKENS, 512)
    zero_index = jnp.zeros((), jnp.int32)

    def one_frame(frame_index):
        group_index = (frame_index // group_frames).astype(jnp.int32)
        ref_frame = (group_index * group_frames + ref_local[group_index]).astype(jnp.int32)
        key_parts = [head_k[frame_index], head_k[ref_frame]]
        value_parts = [head_v[frame_index], head_v[ref_frame]]
        for entry in range(ENTRIES):
            corner = (source[frame_index, entry].astype(jnp.int32), (epi_block[frame_index, entry] * BLOCK).astype(jnp.int32), zero_index, zero_index)
            key_parts.append(lax.dynamic_slice(head_k, corner, (1, BLOCK, HEADS, HEAD_DIM))[0])
            value_parts.append(lax.dynamic_slice(head_v, corner, (1, BLOCK, HEADS, HEAD_DIM))[0])
        key_set = jnp.concatenate(key_parts, 0).astype(jnp.float32)
        value_set = jnp.concatenate(value_parts, 0).astype(jnp.float32)
        live_mask = jnp.concatenate([jnp.ones((2 * TOKENS,), jnp.float32), jnp.repeat(valid[frame_index].astype(jnp.float32), BLOCK)])
        query_blocks = head_q[frame_index].astype(jnp.float32).reshape(TOKENS // block_rows, block_rows, HEADS, HEAD_DIM)

        def per_block(query_block):
            scores = jnp.einsum("qhd,khd->hqk", query_block, key_set) * score_scale
            scores = jnp.where(live_mask > 0, scores, -1e30)
            row_max = jnp.max(scores, axis=-1, keepdims=True)
            weights = jnp.exp(scores - row_max) * live_mask
            weight_sum = jnp.sum(weights, axis=-1)
            probs = lax.optimization_barrier(weights.astype(jnp.bfloat16)).astype(jnp.float32)
            attended = jnp.einsum("hqk,khd->qhd", probs, value_set) / jnp.transpose(weight_sum)[:, :, None]
            return attended.astype(jnp.bfloat16).reshape(block_rows, WIDTH)

        return lax.map(per_block, query_blocks).reshape(TOKENS, WIDTH)

    return lax.map(one_frame, jnp.arange(FRAMES, dtype=jnp.int32))
```

```python
import functools
import math

import jax
import jax.numpy as jnp
from jax import lax
from jax.experimental import pallas as pl
from jax.experimental.pallas import tpu as pltpu
from jax.sharding import PartitionSpec as P

HEADS = 16
HEAD_DIM = 64
BLOCK = 128
FRAMES_DEV = 2
ENTRIES = 6
SPAN = 4


def attend_kernel(
    table_ref, q_ref, pool_ref, out_ref, key_set, value_set, sems, *, inner, n_tok, n_frames
):
    step = pl.program_id(0)
    count = pl.num_programs(0)
    entry_len = n_frames * ENTRIES
    n_blocks = 2 * n_tok + ENTRIES
    outer_index = table_ref[4 * entry_len + n_frames // (SPAN * FRAMES_DEV)]

    def block_place(frame, block):
        ref_block = block - n_tok
        entry = frame * ENTRIES + jnp.maximum(block - 2 * n_tok, 0)
        group = frame // (SPAN * FRAMES_DEV)
        ref_frame = group * (SPAN * FRAMES_DEV) + table_ref[4 * entry_len + group]
        is_own, is_ref = block < n_tok, block < 2 * n_tok
        dev = jnp.where(
            is_own,
            frame // FRAMES_DEV,
            jnp.where(is_ref, ref_frame // FRAMES_DEV, table_ref[entry]),
        )
        place = jnp.where(
            is_own,
            frame % FRAMES_DEV,
            jnp.where(is_ref, ref_frame % FRAMES_DEV, table_ref[entry_len + entry]),
        )
        token_block = jnp.where(
            is_own, block, jnp.where(is_ref, ref_block, table_ref[2 * entry_len + entry])
        )
        return dev // inner, (dev % inner) * n_tok + token_block, place

    def copies(slot, block, source):
        outer, row, place = source
        return (
            pltpu.make_async_copy(
                pool_ref.at[outer, row, place, 0],
                key_set.at[slot, pl.ds(block * BLOCK, BLOCK)],
                sems.at[slot, block, 0],
            ),
            pltpu.make_async_copy(
                pool_ref.at[outer, row, place, 1],
                value_set.at[slot, pl.ds(block * BLOCK, BLOCK)],
                sems.at[slot, block, 1],
            ),
        )

    def fetch(local, slot):
        frame = outer_index * (inner * FRAMES_DEV) + local

        @pl.loop(0, n_blocks)
        def _(block):
            for copy in copies(slot, block, block_place(frame, block)):
                copy.start()

    slot = lax.rem(step, 2)

    @pl.when(step == 0)
    def _():
        fetch(step, slot)

    @pl.when(step + 1 < count)
    def _():
        fetch(step + 1, 1 - slot)

    @pl.loop(0, n_blocks)
    def _(block):
        for copy in copies(slot, block, (0, 0, 0)):
            copy.wait()

    width = q_ref.shape[-1]
    rows = n_tok * BLOCK
    n_keys = n_blocks * BLOCK
    frame = outer_index * (inner * FRAMES_DEV) + step
    position = lax.broadcasted_iota(jnp.int32, (1, n_keys), 1)
    bias = jnp.zeros((1, n_keys), jnp.float32)
    for entry in range(ENTRIES):
        live = table_ref[3 * entry_len + frame * ENTRIES + entry]
        low = 2 * rows + entry * BLOCK
        dead = (position >= low) & (position < low + BLOCK) & (live == 0)
        bias = jnp.where(dead, -1e30, bias)
    block_rows = math.gcd(rows, 256)
    lane_head = lax.broadcasted_iota(jnp.int32, (1, width), 1) // HEAD_DIM
    keys = key_set.at[slot]
    values = value_set.at[slot]
    for first in range(0, n_tok, block_rows // BLOCK):
        query = q_ref[0, first : first + block_rows // BLOCK, 0].reshape(block_rows, width)
        query = query * jnp.asarray(HEAD_DIM**-0.5, query.dtype)
        result = jnp.zeros((block_rows, width), jnp.float32)
        for head in range(width // HEAD_DIM):
            mine = lane_head == head
            head_query = jnp.where(mine, query, jnp.zeros_like(query))
            scores = lax.dot_general(
                head_query, keys[...], (((1,), (1,)), ((), ())), preferred_element_type=jnp.float32
            )
            scores = scores + bias
            weights = jnp.exp(scores - jnp.max(scores, axis=-1, keepdims=True))
            weight_sum = jnp.sum(weights, axis=-1, keepdims=True)
            attended = jnp.dot(
                weights.astype(jnp.bfloat16), values[...], preferred_element_type=jnp.float32
            )
            result = jnp.where(mine, attended / weight_sum, result)
        out_ref[0, first : first + block_rows // BLOCK, 0] = result.astype(out_ref.dtype).reshape(
            block_rows // BLOCK, BLOCK, width
        )


def attend(table, query, pool, inner, n_tok, n_frames):
    n_local = inner * FRAMES_DEV
    width = query.shape[-1]
    n_blocks = 2 * n_tok + ENTRIES
    frame_spec = pl.BlockSpec(
        (1, n_tok, 1, BLOCK, width), lambda g, t: (g // FRAMES_DEV, 0, g % FRAMES_DEV, 0, 0)
    )
    key_rows = n_blocks * BLOCK
    flops = 4 * n_local * n_tok * BLOCK * key_rows * width
    return pl.pallas_call(
        functools.partial(attend_kernel, inner=inner, n_tok=n_tok, n_frames=n_frames),
        out_shape=jax.ShapeDtypeStruct(query.shape, query.dtype),
        grid_spec=pltpu.PrefetchScalarGridSpec(
            num_scalar_prefetch=1,
            grid=(n_local,),
            in_specs=[frame_spec, pl.BlockSpec(memory_space=pl.ANY)],
            out_specs=frame_spec,
            scratch_shapes=[
                pltpu.VMEM((2, key_rows, width), query.dtype),
                pltpu.VMEM((2, key_rows, width), query.dtype),
                pltpu.SemaphoreType.DMA((2, n_blocks, 2)),
            ],
        ),
        compiler_params=pltpu.CompilerParams(vmem_limit_bytes=48 * 1024 * 1024),
        cost_estimate=pl.CostEstimate(
            flops=flops,
            bytes_accessed=4 * n_local * key_rows * width + 4 * query.size,
            transcendentals=flops // (4 * HEAD_DIM),
        ),
    )(table, query, pool)


def shards(queries, keys, values, epi_dev, epi_frame, epi_block, valid, ref_local, *, n_tm, n_tok):
    inner = math.gcd(SPAN, max(1, HEADS // n_tok))
    n_outer = n_tm // inner
    n_ranks = inner * n_tok
    width = keys.shape[2] // n_ranks
    n_frames = epi_dev.shape[0]
    plane_groups = [
        [(o * inner + i) * n_tok + t for i in range(inner) for t in range(n_tok)]
        for o in range(n_outer)
    ]
    outer_groups = [[o * inner + i for o in range(n_outer)] for i in range(inner)]

    def to_heads(x):
        return lax.all_to_all(
            x, ("tm", "tok"), 0, 0, axis_index_groups=plane_groups, tiled=True
        )

    my_outer = lax.axis_index("tm") // inner
    table = jnp.concatenate(
        [a.reshape(-1) for a in (epi_dev, epi_frame, epi_block, valid, ref_local)]
        + [my_outer.reshape(1).astype(jnp.int32)]
    )
    pair = jnp.stack([keys, values]).reshape(2, FRAMES_DEV, BLOCK, n_ranks, width)
    own = to_heads(pair.transpose(3, 1, 0, 2, 4))
    pool = lax.all_gather(own, "tm", axis=0, axis_index_groups=outer_groups)
    query = to_heads(queries.reshape(FRAMES_DEV, BLOCK, n_ranks, width).transpose(2, 0, 1, 3))
    query = query.reshape(inner, n_tok, FRAMES_DEV, BLOCK, width)
    attended = attend(table, query, pool, inner, n_tok, n_frames)
    attended = to_heads(attended.reshape(n_ranks, FRAMES_DEV, BLOCK, width))
    return attended.transpose(1, 2, 0, 3).reshape(queries.shape)


def solution(mesh):
    return jax.shard_map(
        functools.partial(shards, n_tm=mesh.shape["tm"], n_tok=mesh.shape["tok"]),
        mesh=mesh,
        in_specs=(P("tm", "tok", None),) * 3 + (P(),) * 5,
        out_specs=P("tm", "tok", None),
        check_vma=False,
    )
```

```python
import functools
import math

import jax
import jax.numpy as jnp
from jax import lax
from jax.experimental import pallas as pl
from jax.experimental.pallas import tpu as pltpu
from jax.sharding import PartitionSpec as P

HEADS = 16
HEAD_DIM = 64
BLOCK = 128
FRAMES_DEV = 2
ENTRIES = 6
SPAN = 4


def attend_kernel(
    table_ref, plan_ref, q_ref, *refs, inner, n_tok, n_frames, spot_row
):
    buffers, (out_ref, key_set, value_set, sems) = refs[:-4], refs[-4:]
    key_buffers, value_buffers = buffers[::2], buffers[1::2]
    step = pl.program_id(0)
    count = pl.num_programs(0)
    units = inner * n_tok * FRAMES_DEV
    entry_len = n_frames * ENTRIES
    n_blocks = 2 * n_tok + ENTRIES
    outer_index = table_ref[4 * entry_len + n_frames // (SPAN * FRAMES_DEV)]

    def block_place(frame, block):
        ref_block = block - n_tok
        entry = frame * ENTRIES + jnp.maximum(block - 2 * n_tok, 0)
        group = frame // (SPAN * FRAMES_DEV)
        ref_frame = group * (SPAN * FRAMES_DEV) + table_ref[4 * entry_len + group]
        is_own, is_ref = block < n_tok, block < 2 * n_tok
        dev = jnp.where(
            is_own,
            frame // FRAMES_DEV,
            jnp.where(is_ref, ref_frame // FRAMES_DEV, table_ref[entry]),
        )
        place = jnp.where(
            is_own,
            frame % FRAMES_DEV,
            jnp.where(is_ref, ref_frame % FRAMES_DEV, table_ref[entry_len + entry]),
        )
        token_block = jnp.where(
            is_own, block, jnp.where(is_ref, ref_block, table_ref[2 * entry_len + entry])
        )
        unit = ((dev % inner) * n_tok + token_block) * FRAMES_DEV + place
        outer = dev // inner
        return jnp.where(outer == outer_index, unit, plan_ref[spot_row, outer * units + unit])

    def copies(slot, block, index, spot):
        rows = pl.ds(block * BLOCK, BLOCK)
        return (
            pltpu.make_async_copy(
                key_buffers[index].at[spot], key_set.at[slot, rows], sems.at[slot, block, 0]
            ),
            pltpu.make_async_copy(
                value_buffers[index].at[spot], value_set.at[slot, rows], sems.at[slot, block, 1]
            ),
        )

    def fetch(local, slot):
        frame = outer_index * (inner * FRAMES_DEV) + local

        @pl.loop(0, n_blocks)
        def _(block):
            code = block_place(frame, block)
            for index in range(len(key_buffers)):

                @pl.when(code // 1024 == index)
                def _():
                    for copy in copies(slot, block, index, code % 1024):
                        copy.start()

    slot = lax.rem(step, 2)

    @pl.when(step == 0)
    def _():
        fetch(step, slot)

    @pl.when(step + 1 < count)
    def _():
        fetch(step + 1, 1 - slot)

    @pl.loop(0, n_blocks)
    def _(block):
        for copy in copies(slot, block, 0, 0):
            copy.wait()

    width = q_ref.shape[-1]
    rows = n_tok * BLOCK
    n_keys = n_blocks * BLOCK
    frame = outer_index * (inner * FRAMES_DEV) + step
    position = lax.broadcasted_iota(jnp.int32, (1, n_keys), 1)
    bias = jnp.zeros((1, n_keys), jnp.float32)
    for entry in range(ENTRIES):
        live = table_ref[3 * entry_len + frame * ENTRIES + entry]
        low = 2 * rows + entry * BLOCK
        dead = (position >= low) & (position < low + BLOCK) & (live == 0)
        bias = jnp.where(dead, -1e30, bias)
    block_rows = math.gcd(rows, 256)
    lane_head = lax.broadcasted_iota(jnp.int32, (1, width), 1) // HEAD_DIM
    keys = key_set.at[slot]
    values = value_set.at[slot]
    for first in range(0, n_tok, block_rows // BLOCK):
        query = q_ref[0, first : first + block_rows // BLOCK, 0].reshape(block_rows, width)
        query = query * jnp.asarray(HEAD_DIM**-0.5, query.dtype)
        result = jnp.zeros((block_rows, width), jnp.float32)
        for head in range(width // HEAD_DIM):
            mine = lane_head == head
            head_query = jnp.where(mine, query, jnp.zeros_like(query))
            scores = lax.dot_general(
                head_query, keys[...], (((1,), (1,)), ((), ())), preferred_element_type=jnp.float32
            )
            scores = scores + bias
            weights = jnp.exp(scores - jnp.max(scores, axis=-1, keepdims=True))
            weight_sum = jnp.sum(weights, axis=-1, keepdims=True)
            attended = jnp.dot(
                weights.astype(jnp.bfloat16), values[...], preferred_element_type=jnp.float32
            )
            result = jnp.where(mine, attended / weight_sum, result)
        out_ref[0, first : first + block_rows // BLOCK, 0] = result.astype(out_ref.dtype).reshape(
            block_rows // BLOCK, BLOCK, width
        )


def attend(table, plan, query, buffers, inner, n_tok, n_frames, spot_row):
    n_local = inner * FRAMES_DEV
    width = query.shape[-1]
    n_blocks = 2 * n_tok + ENTRIES
    frame_spec = pl.BlockSpec(
        (1, n_tok, 1, BLOCK, width), lambda g, *_: (g // FRAMES_DEV, 0, g % FRAMES_DEV, 0, 0)
    )
    key_rows = n_blocks * BLOCK
    flops = 4 * n_local * n_tok * BLOCK * key_rows * width
    return pl.pallas_call(
        functools.partial(
            attend_kernel, inner=inner, n_tok=n_tok, n_frames=n_frames, spot_row=spot_row
        ),
        out_shape=jax.ShapeDtypeStruct(query.shape, query.dtype),
        grid_spec=pltpu.PrefetchScalarGridSpec(
            num_scalar_prefetch=2,
            grid=(n_local,),
            in_specs=[frame_spec] + [pl.BlockSpec(memory_space=pl.ANY)] * len(buffers),
            out_specs=frame_spec,
            scratch_shapes=[
                pltpu.VMEM((2, key_rows, width), query.dtype),
                pltpu.VMEM((2, key_rows, width), query.dtype),
                pltpu.SemaphoreType.DMA((2, n_blocks, 2)),
            ],
        ),
        compiler_params=pltpu.CompilerParams(vmem_limit_bytes=48 * 1024 * 1024),
        cost_estimate=pl.CostEstimate(
            flops=flops,
            bytes_accessed=4 * n_local * key_rows * width + 4 * query.size,
            transcendentals=flops // (4 * HEAD_DIM),
        ),
    )(table, plan, query, *buffers)


def plan_kernel(
    me_ref, ref_ref, dev_ref, place_ref, block_ref, valid_ref, out_ref, *, inner, n_tok, rounds, room
):
    n_frames = dev_ref.shape[0]
    units = inner * n_tok * FRAMES_DEV
    plane_frames = inner * FRAMES_DEV
    n_outer = n_frames // plane_frames
    lanes = out_ref.shape[1]
    f32 = jnp.float32
    me = me_ref[0].astype(f32)
    dev, place = dev_ref[...], place_ref[...]
    ids = (dev // inner) * units + ((dev % inner) * n_tok + block_ref[...]) * FRAMES_DEV + place
    used = valid_ref[...] > 0
    frame_lane = lax.broadcasted_iota(jnp.int32, (n_frames, lanes), 1)
    hit = jnp.zeros((n_frames, lanes), f32)
    for entry in range(ENTRIES):
        here = (ids[:, entry : entry + 1] == frame_lane) & used[:, entry : entry + 1]
        hit = jnp.where(here, 1.0, hit)
    lane = lax.broadcasted_iota(jnp.int32, (1, lanes), 1)
    unit = lane % units
    origin = (lane // units).astype(f32)
    need = []
    for plane in range(n_outer):
        rows = lax.slice_in_dim(hit, plane * plane_frames, (plane + 1) * plane_frames)
        wanted = jnp.max(rows, axis=0, keepdims=True) > 0
        if inner % SPAN:
            group = plane * inner // SPAN
            ref_frame = group * (SPAN * FRAMES_DEV) + ref_ref[group]
            ref_dev = ref_frame // FRAMES_DEV
            wanted = wanted | (
                (lane // (n_tok * FRAMES_DEV) == ref_dev)
                & (lane % FRAMES_DEV == ref_frame % FRAMES_DEV)
            )
        need.append(wanted)

    square_row = lax.broadcasted_iota(jnp.int32, (lanes, lanes), 0)
    square_lane = lax.broadcasted_iota(jnp.int32, (lanes, lanes), 1)
    diagonal = square_row == square_lane
    earlier = square_row < square_lane

    def column(row):
        return jnp.sum(jnp.where(diagonal, row, 0.0), axis=1, keepdims=True)

    def count(mask, axis):
        return jnp.sum(jnp.where(mask, 1.0, 0.0), axis=axis, keepdims=True)

    def one_way(start, reach, here):
        start_col, reach_col = column(start), column(reach)
        ahead = (reach_col > reach) | ((reach_col == reach) & earlier)
        rank = count((start_col == start) & (reach_col > 0) & ahead, 0)
        depart = jnp.zeros_like(start)
        for plane in range(n_outer - 1, 0, -1):
            total = jnp.zeros((1, 1), f32)
            turn = jnp.ones_like(start)
            for step in range(1, rounds + 1):
                if plane < n_outer - 1:
                    passing = (
                        (start > plane)
                        & (start - reach <= plane - 1)
                        & (depart + (start - plane) == step)
                        & (reach > 0)
                    )
                    total = total + (room - count(passing, 1))
                else:
                    total = total + room
                turn = turn + jnp.where(total <= rank, 1.0, 0.0)
            depart = jnp.where((start == plane) & (reach > 0), turn, depart)
        last = jnp.max(jnp.where(reach > 0, depart + reach - 1.0, 0.0), axis=1, keepdims=True)

        def on_link(link):
            crosses = (reach > 0) & (start > link) & (start - reach <= link)
            step = jnp.where(crosses, depart + (start - 1.0 - link), -1.0)
            slot = count((column(step) == step) & earlier, 0)
            return crosses, step, slot

        arrives, in_step, in_slot = on_link(here)
        leaves, out_step, out_slot = on_link(here - 1.0)
        source = jnp.where(start == here, unit.astype(f32), units + in_slot)
        key = column(jnp.where(leaves, (out_step - 1.0) * room + out_slot, -1.0))
        sent = jnp.sum(
            jnp.where(key == square_lane.astype(f32), column(source), 0.0), axis=0, keepdims=True
        )
        return arrives, in_step, in_slot, sent, last

    lowest, highest = origin, origin
    for plane in range(n_outer):
        highest = jnp.where(need[plane] & (origin < plane), float(plane), highest)
        other = n_outer - 1 - plane
        lowest = jnp.where(need[other] & (origin > other), float(other), lowest)
    top = n_outer - 1.0
    down = one_way(origin, origin - lowest, me)
    up = one_way(top - origin, highest - origin, top - me)
    unit_f = unit.astype(f32)
    spots = unit_f
    for way, (arrives, in_step, in_slot, _, _) in enumerate((down, up)):
        spots = jnp.where(arrives, (in_step + way * rounds) * 1024 + in_slot, spots)
    distance = origin - me
    full = jnp.where(distance > 0, distance, jnp.where(distance < 0, n_outer - 1 - distance, 0))
    last = jnp.maximum(down[4], up[4]) + jnp.zeros_like(origin)
    rows = [spots, down[3], up[3], full * 1024 + unit_f, last]
    for index, row in enumerate(rows):
        out_ref[index : index + 1, :] = row.astype(jnp.int32)


def make_plan(epi_dev, epi_frame, epi_block, valid, ref_local, my_outer, inner, n_tok, rounds, room):
    n_blocks = epi_dev.shape[0] * n_tok
    lanes = -(-n_blocks // 128) * 128
    smem, vmem = pl.BlockSpec(memory_space=pltpu.SMEM), pl.BlockSpec(memory_space=pltpu.VMEM)
    return pl.pallas_call(
        functools.partial(plan_kernel, inner=inner, n_tok=n_tok, rounds=rounds, room=room),
        out_shape=jax.ShapeDtypeStruct((8, lanes), jnp.int32),
        in_specs=[smem, smem, vmem, vmem, vmem, vmem],
        out_specs=vmem,
        compiler_params=pltpu.CompilerParams(vmem_limit_bytes=32 * 1024 * 1024),
    )(my_outer.reshape(1), ref_local, epi_dev, epi_frame, epi_block, valid)


def pack_kernel(plan_ref, *refs, step, room, units):
    sources, targets = refs[:-2], refs[-2:]
    own = sources[0]
    for way, target in enumerate(targets):
        for slot in range(room):
            code = plan_ref[1 + way, (step - 1) * room + slot]
            if step == 1:
                target[slot] = own[code]
            else:

                @pl.when(code < units)
                def _():
                    target[slot] = own[code]

                @pl.when(code >= units)
                def _():
                    target[slot] = sources[1 + way][code - units]


def pack(plan, own, previous, step, room):
    out = jax.ShapeDtypeStruct((room,) + own.shape[1:], own.dtype)
    whole = pl.BlockSpec(memory_space=pltpu.VMEM)
    return pl.pallas_call(
        functools.partial(pack_kernel, step=step, room=room, units=own.shape[0]),
        out_shape=(out, out),
        grid_spec=pltpu.PrefetchScalarGridSpec(
            num_scalar_prefetch=1,
            grid=(),
            in_specs=[whole] * (1 + len(previous)),
            out_specs=(whole, whole),
        ),
        compiler_params=pltpu.CompilerParams(vmem_limit_bytes=16 * 1024 * 1024),
        cost_estimate=pl.CostEstimate(
            flops=0, bytes_accessed=8 * math.prod(out.shape), transcendentals=0
        ),
    )(plan, own, *previous)


def shards(queries, keys, values, epi_dev, epi_frame, epi_block, valid, ref_local, *, n_tm, n_tok):
    inner = math.gcd(SPAN, max(1, HEADS // n_tok))
    n_outer = n_tm // inner
    n_ranks = inner * n_tok
    units = n_ranks * FRAMES_DEV
    width = keys.shape[2] // n_ranks
    n_frames = epi_dev.shape[0]
    rounds, room = n_outer - 1, -(-units * 5 // 8)
    plane_groups = [
        [(o * inner + i) * n_tok + t for i in range(inner) for t in range(n_tok)]
        for o in range(n_outer)
    ]

    def exchange(x):
        return lax.all_to_all(
            x, ("tm", "tok"), 0, 0, axis_index_groups=plane_groups, tiled=True
        )

    def to_heads(x):
        return exchange(
            x.reshape(FRAMES_DEV, BLOCK, n_ranks, width).transpose(2, 0, 1, 3)
        )

    def shift(x, way):
        pairs = [
            (o * inner + i, (o + way) * inner + i)
            for o in range(n_outer)
            for i in range(inner)
            if 0 <= o + way < n_outer
        ]
        return lax.ppermute(x, "tm", pairs)

    my_outer = (lax.axis_index("tm") // inner).astype(jnp.int32)
    table = jnp.concatenate(
        [a.reshape(-1) for a in (epi_dev, epi_frame, epi_block, valid, ref_local)]
        + [my_outer.reshape(1)]
    )
    plan = make_plan(
        epi_dev, epi_frame, epi_block, valid, ref_local, my_outer, inner, n_tok, rounds, room
    )
    own_keys = to_heads(keys).reshape(units, BLOCK, width)
    own_values = to_heads(values).reshape(units, BLOCK, width)
    query = to_heads(queries).reshape(inner, n_tok, FRAMES_DEV, BLOCK, width)

    def finish(query, own, down, up, spot_row):
        buffers = [own] + down + up
        flat = [array for pair in buffers for array in pair]
        attended = attend(table, plan, query, flat, inner, n_tok, n_frames, spot_row)
        attended = exchange(attended.reshape(n_ranks, FRAMES_DEV, BLOCK, width))
        return attended.transpose(1, 2, 0, 3).reshape(queries.shape)

    def listed(query, own_keys, own_values):
        got = {}
        for step in range(1, rounds + 1):
            for kind, own in enumerate((own_keys, own_values)):
                previous = [got[kind, way, step - 1] for way in (0, 1)] if step > 1 else []
                sent = pack(plan, own, previous, step, room)
                for way in (0, 1):
                    got[kind, way, step] = shift(sent[way], 2 * way - 1)
        received = [
            [(got[0, way, step], got[1, way, step]) for step in range(1, rounds + 1)]
            for way in (0, 1)
        ]
        return finish(query, (own_keys, own_values), *received, 0)

    def gathered(query, own_keys, own_values):
        received = ([], [])
        for way in (0, 1):
            pair = (own_keys, own_values)
            for _ in range(n_outer - 1):
                pair = tuple(shift(array, 2 * way - 1) for array in pair)
                received[way].append(pair)
        return finish(query, (own_keys, own_values), *received, 3)

    return lax.cond(plan[4, 0] <= rounds, listed, gathered, query, own_keys, own_values)


def solution(mesh):
    return jax.shard_map(
        functools.partial(shards, n_tm=mesh.shape["tm"], n_tok=mesh.shape["tok"]),
        mesh=mesh,
        in_specs=(P("tm", "tok", None),) * 3 + (P(),) * 5,
        out_specs=P("tm", "tok", None),
        check_vma=False,
    )
```

```python
import functools
import math

import jax
import jax.numpy as jnp
from jax import lax
from jax.experimental import pallas as pl
from jax.experimental.pallas import tpu as pltpu
from jax.sharding import PartitionSpec as P

HEADS = 16
HEAD_DIM = 64
BLOCK = 128
FRAMES_DEV = 2
ENTRIES = 6
SPAN = 4


def plan_kernel(
    me_ref, ref_ref, dev_hbm, place_hbm, block_hbm, valid_hbm, out_ref, entries, sems,
    *, inner, n_tok, rounds, room,
):
    copies = [
        pltpu.make_async_copy(array, entries.at[index], sems.at[index])
        for index, array in enumerate((dev_hbm, place_hbm, block_hbm, valid_hbm))
    ]
    for copy in copies:
        copy.start()
    for copy in copies:
        copy.wait()
    n_frames = dev_hbm.shape[0]
    units = inner * n_tok * FRAMES_DEV
    plane_frames = inner * FRAMES_DEV
    n_outer = n_frames // plane_frames
    lanes = out_ref.shape[1]
    f32 = jnp.float32
    me = me_ref[0].astype(f32)
    dev, place = entries[0], entries[1]
    ids = (dev // inner) * units + ((dev % inner) * n_tok + entries[2]) * FRAMES_DEV + place
    used = entries[3] > 0
    frame_lane = lax.broadcasted_iota(jnp.int32, (n_frames, lanes), 1)
    hit = jnp.zeros((n_frames, lanes), f32)
    for entry in range(ENTRIES):
        here = (ids[:, entry : entry + 1] == frame_lane) & used[:, entry : entry + 1]
        hit = jnp.where(here, 1.0, hit)
    lane = lax.broadcasted_iota(jnp.int32, (1, lanes), 1)
    unit = lane % units
    origin = (lane // units).astype(f32)
    need = []
    for plane in range(n_outer):
        rows = lax.slice_in_dim(hit, plane * plane_frames, (plane + 1) * plane_frames)
        wanted = jnp.max(rows, axis=0, keepdims=True) > 0
        if inner % SPAN:
            group = plane * inner // SPAN
            ref_frame = group * (SPAN * FRAMES_DEV) + ref_ref[group]
            ref_dev = ref_frame // FRAMES_DEV
            wanted = wanted | (
                (lane // (n_tok * FRAMES_DEV) == ref_dev)
                & (lane % FRAMES_DEV == ref_frame % FRAMES_DEV)
            )
        need.append(wanted)

    square_row = lax.broadcasted_iota(jnp.int32, (lanes, lanes), 0)
    square_lane = lax.broadcasted_iota(jnp.int32, (lanes, lanes), 1)
    diagonal = square_row == square_lane
    earlier = square_row < square_lane

    def column(row):
        return jnp.sum(jnp.where(diagonal, row, 0.0), axis=1, keepdims=True)

    def count(mask, axis):
        return jnp.sum(jnp.where(mask, 1.0, 0.0), axis=axis, keepdims=True)

    def one_way(start, reach, here):
        start_col, reach_col = column(start), column(reach)
        ahead = (reach_col > reach) | ((reach_col == reach) & earlier)
        rank = count((start_col == start) & (reach_col > 0) & ahead, 0)
        depart = jnp.zeros_like(start)
        for plane in range(n_outer - 1, 0, -1):
            total = jnp.zeros((1, 1), f32)
            turn = jnp.ones_like(start)
            for step in range(1, rounds + 1):
                if plane < n_outer - 1:
                    passing = (
                        (start > plane)
                        & (start - reach <= plane - 1)
                        & (depart + (start - plane) == step)
                        & (reach > 0)
                    )
                    total = total + (room - count(passing, 1))
                else:
                    total = total + room
                turn = turn + jnp.where(total <= rank, 1.0, 0.0)
            depart = jnp.where((start == plane) & (reach > 0), turn, depart)
        last = jnp.max(jnp.where(reach > 0, depart + reach - 1.0, 0.0), axis=1, keepdims=True)

        def on_link(link):
            crosses = (reach > 0) & (start > link) & (start - reach <= link)
            step = jnp.where(crosses, depart + (start - 1.0 - link), -1.0)
            slot = count((column(step) == step) & earlier, 0)
            return crosses, step, slot

        arrives, in_step, in_slot = on_link(here)
        leaves, out_step, out_slot = on_link(here - 1.0)
        source = jnp.where(start == here, unit.astype(f32), units + in_slot)
        key = column(jnp.where(leaves, (out_step - 1.0) * room + out_slot, -1.0))
        sent = jnp.sum(
            jnp.where(key == square_lane.astype(f32), column(source), 0.0), axis=0, keepdims=True
        )
        return arrives, in_step, in_slot, sent, last

    lowest, highest = origin, origin
    for plane in range(n_outer):
        highest = jnp.where(need[plane] & (origin < plane), float(plane), highest)
        other = n_outer - 1 - plane
        lowest = jnp.where(need[other] & (origin > other), float(other), lowest)
    top = n_outer - 1.0
    down = one_way(origin, origin - lowest, me)
    up = one_way(top - origin, highest - origin, top - me)
    unit_f = unit.astype(f32)
    spots = unit_f
    for way, (arrives, in_step, in_slot, _, _) in enumerate((down, up)):
        spots = jnp.where(arrives, (in_step + way * rounds) * 1024 + in_slot, spots)
    distance = origin - me
    full = jnp.where(distance > 0, distance, jnp.where(distance < 0, n_outer - 1 - distance, 0))
    last = jnp.maximum(down[4], up[4]) + jnp.zeros_like(origin)
    full = full * 1024 + unit_f
    first = me * plane_frames
    row_frame = lax.broadcasted_iota(jnp.int32, (n_frames, lanes), 0).astype(f32)
    wide_lane = frame_lane.astype(f32)
    group = me_ref[0] * inner // SPAN
    ref_frame = group * (SPAN * FRAMES_DEV) + ref_ref[group]
    ref_dev = ref_frame // FRAMES_DEV

    def places(table):
        listed = jnp.zeros((1, lanes), f32)
        for entry in range(ENTRIES):
            mine, live = ids[:, entry : entry + 1], used[:, entry : entry + 1]
            found = jnp.sum(jnp.where(mine == frame_lane, table, 0.0), axis=1, keepdims=True)
            found = jnp.where(live, found, 65536.0)
            target = (row_frame - first) * 8 + entry
            listed += jnp.sum(jnp.where(target == wide_lane, found, 0.0), axis=0, keepdims=True)
        listed = jnp.where(lane % 8 < ENTRIES, listed, 65536.0)
        refs = jnp.zeros((1, lanes), f32)
        for block in range(n_tok):
            which = (ref_dev * n_tok + block) * FRAMES_DEV + ref_frame % FRAMES_DEV
            found = jnp.sum(jnp.where(lane == which, table, 0.0), axis=1, keepdims=True)
            refs = jnp.where(lane == block, found, refs)
        return [listed, refs]

    last = jnp.maximum(down[4], up[4]) + jnp.zeros_like(origin)
    rows = [down[3], up[3], last] + places(spots) + places(full)
    for index, row in enumerate(rows):
        out_ref[index : index + 1, :] = row.astype(jnp.int32)


def make_plan(epi_dev, epi_frame, epi_block, valid, ref_local, my_outer, inner, n_tok, rounds, room):
    n_blocks = epi_dev.shape[0] * n_tok
    lanes = -(-n_blocks // 128) * 128
    smem, anywhere = pl.BlockSpec(memory_space=pltpu.SMEM), pl.BlockSpec(memory_space=pl.ANY)
    return pl.pallas_call(
        functools.partial(plan_kernel, inner=inner, n_tok=n_tok, rounds=rounds, room=room),
        out_shape=jax.ShapeDtypeStruct((8, lanes), jnp.int32),
        in_specs=[smem, smem] + [anywhere] * 4,
        out_specs=pl.BlockSpec(memory_space=pltpu.VMEM),
        scratch_shapes=[
            pltpu.VMEM((4,) + epi_dev.shape, jnp.int32),
            pltpu.SemaphoreType.DMA((4,)),
        ],
        compiler_params=pltpu.CompilerParams(vmem_limit_bytes=32 * 1024 * 1024),
    )(my_outer.reshape(1), ref_local, epi_dev, epi_frame, epi_block, valid)


def pack_kernel(plan_ref, *refs, step, room, units):
    sources, targets = refs[:-2], refs[-2:]
    own = sources[0]
    for way, target in enumerate(targets):
        for slot in range(room):
            code = plan_ref[way, (step - 1) * room + slot]
            if step == 1:
                target[slot] = own[code, 1:3]
            else:

                @pl.when(code < units)
                def _():
                    target[slot] = own[code, 1:3]

                @pl.when(code >= units)
                def _():
                    target[slot] = sources[1 + way][code - units]


def pack(plan, own, previous, step, room):
    out = jax.ShapeDtypeStruct((room, 2) + own.shape[2:], own.dtype)
    whole = pl.BlockSpec(memory_space=pltpu.VMEM)
    return pl.pallas_call(
        functools.partial(pack_kernel, step=step, room=room, units=own.shape[0]),
        out_shape=(out, out),
        grid_spec=pltpu.PrefetchScalarGridSpec(
            num_scalar_prefetch=1,
            grid=(),
            in_specs=[whole] * (1 + len(previous)),
            out_specs=(whole, whole),
        ),
        compiler_params=pltpu.CompilerParams(vmem_limit_bytes=24 * 1024 * 1024),
        cost_estimate=pl.CostEstimate(
            flops=0, bytes_accessed=8 * math.prod(out.shape), transcendentals=0
        ),
    )(plan, own, *previous)


def fold(keys, values, query, acc, stat, fresh):
    width, tile = acc.shape
    scores = jnp.dot(keys, query, preferred_element_type=jnp.float32)
    top = jnp.max(scores, axis=0, keepdims=True)
    if not fresh:
        old_top = stat[0:1]
        top = jnp.maximum(old_top, top)
    weights = jnp.exp(scores - top)
    total = jnp.sum(weights, axis=0, keepdims=True)
    weights = weights.astype(jnp.bfloat16)
    if not fresh:
        keep = jnp.exp(old_top - top)
        total = stat[1:2] * keep + total
    stat[0:1] = top
    stat[1:2] = total
    channels = values.T
    for head in range(width // HEAD_DIM):
        rows, lanes = pl.ds(head * HEAD_DIM, HEAD_DIM), slice(head * tile, (head + 1) * tile)
        attended = jnp.dot(
            channels[head * HEAD_DIM : (head + 1) * HEAD_DIM],
            weights[:, lanes],
            preferred_element_type=jnp.float32,
        )
        acc[rows] = attended if fresh else acc[rows] * keep[:, lanes] + attended


def listed_items(plan_ref, sources, block_set, query_ref, acc_ref, stat_ref, spot_row, n_refs):
    n_local, n_tiles = acc_ref.shape[:2]

    def item(local, code):
        spot, origin = code & 1023, code >> 10
        for number, (source, first) in sources.items():

            @pl.when(origin == number)
            def _():
                block_set[...] = source[spot, first : first + 2]

        hit = functools.reduce(jnp.logical_or, [origin == number for number in sources])

        @pl.when(hit)
        def _():
            for tile in range(n_tiles):
                fold(
                    block_set[0], block_set[1], query_ref[local, tile], acc_ref.at[local, tile],
                    stat_ref.at[local, tile], False,
                )

    @pl.loop(0, n_local * 8)
    def _(index):
        item(index >> 3, plan_ref[spot_row, index])

    if n_refs:

        @pl.loop(0, n_local * n_refs)
        def _(index):
            item(lax.div(index, n_refs), plan_ref[spot_row + 1, lax.rem(index, n_refs)])


def near_kernel(plan_ref, own_ref, query_ref, acc_ref, stat_ref, block_set, *, n_tok, spot_row, ref_near):
    n_local, n_tiles, width, tile = acc_ref.shape
    heads = width // HEAD_DIM
    row_head = lax.broadcasted_iota(jnp.int32, (width, 1), 0) // HEAD_DIM

    @pl.loop(0, n_local, unroll=2)
    def _(local):
        base = (local // FRAMES_DEV) * (n_tok * FRAMES_DEV) + local % FRAMES_DEV
        spots = [base + block * FRAMES_DEV for block in range(n_tok)]
        blocks = [own_ref.at[spot] for spot in spots]
        if ref_near:
            blocks += [own_ref.at[plan_ref[spot_row + 1, block]] for block in range(n_tok)]
        keys = jnp.concatenate([block[1] for block in blocks], 0)
        values = jnp.concatenate([block[2] for block in blocks], 0)
        for index in range(n_tiles):
            first = index * tile // BLOCK
            turned = jnp.concatenate(
                [own_ref[spot, 0].T for spot in spots[first : first + tile // BLOCK]], 1
            )
            turned = turned * jnp.asarray(HEAD_DIM**-0.5, turned.dtype)
            query = jnp.concatenate(
                [jnp.where(row_head == head, turned, jnp.zeros_like(turned)) for head in range(heads)],
                1,
            )
            query_ref[local, index] = query
            fold(keys, values, query, acc_ref.at[local, index], stat_ref.at[local, index], True)

    listed_items(
        plan_ref, {0: (own_ref, 1)}, block_set, query_ref, acc_ref, stat_ref, spot_row,
        0 if ref_near else n_tok,
    )


def near(plan, own, n_local, n_tok, spot_row, ref_near):
    width = own.shape[-1]
    rows = n_tok * BLOCK
    tile = math.gcd(rows, 256)
    lanes = tile * (width // HEAD_DIM)
    whole = pl.BlockSpec(memory_space=pltpu.VMEM)
    pairs = n_local * rows * (1 + ref_near) * rows
    return pl.pallas_call(
        functools.partial(near_kernel, n_tok=n_tok, spot_row=spot_row, ref_near=ref_near),
        out_shape=(
            jax.ShapeDtypeStruct((n_local, rows // tile, width, lanes), own.dtype),
            jax.ShapeDtypeStruct((n_local, rows // tile, width, tile), jnp.float32),
            jax.ShapeDtypeStruct((n_local, rows // tile, 2, lanes), jnp.float32),
        ),
        grid_spec=pltpu.PrefetchScalarGridSpec(
            num_scalar_prefetch=1,
            grid=(),
            in_specs=[whole],
            out_specs=(whole, whole, whole),
            scratch_shapes=[pltpu.VMEM((2, BLOCK, width), own.dtype)],
        ),
        compiler_params=pltpu.CompilerParams(vmem_limit_bytes=40 * 1024 * 1024),
        cost_estimate=pl.CostEstimate(
            flops=4 * pairs * width,
            bytes_accessed=16 * n_local * rows * width,
            transcendentals=pairs * width // HEAD_DIM,
        ),
    )(plan, own)


def stage_kernel(
    plan_ref, down_ref, up_ref, query_ref, acc_in, stat_in, acc_ref, *refs, numbers, spot_row, n_refs, final
):
    stat_ref, block_set = refs[-2:]
    if final:
        out_ref, acc_ref = acc_ref, refs[0]
    sources = {numbers[0]: (down_ref, 0), numbers[1]: (up_ref, 0)}
    listed_items(plan_ref, sources, block_set, query_ref, acc_ref, stat_ref, spot_row, n_refs)
    if not final:
        return
    n_local, n_tiles, width, tile = acc_ref.shape
    n_tok = n_tiles * tile // BLOCK
    row_head = lax.broadcasted_iota(jnp.int32, (width, 1), 0) // HEAD_DIM

    @pl.loop(0, n_local, unroll=2)
    def _(local):
        for index in range(n_tiles):
            total = stat_ref[local, index][1:2]
            share = 1.0 / total[:, :tile]
            for head in range(1, width // HEAD_DIM):
                other = 1.0 / total[:, head * tile : (head + 1) * tile]
                share = jnp.where(row_head == head, other, share)
            result = (acc_ref[local, index] * share).T.astype(out_ref.dtype)
            for block in range(tile // BLOCK):
                rank = (local // FRAMES_DEV) * n_tok + index * (tile // BLOCK) + block
                out_ref[rank, local % FRAMES_DEV] = result[block * BLOCK : (block + 1) * BLOCK]


def stage(plan, received, query, acc, stat, numbers, n_ranks, spot_row, n_refs, final):
    width = acc.shape[2]
    whole = pl.BlockSpec(memory_space=pltpu.VMEM)
    out_shape = [jax.ShapeDtypeStruct(x.shape, x.dtype) for x in (acc, stat)]
    if final:
        out_shape = [
            jax.ShapeDtypeStruct((n_ranks, FRAMES_DEV, BLOCK, width), query.dtype)
        ] + out_shape
    pairs = 2 * acc.size // width * BLOCK
    return pl.pallas_call(
        functools.partial(
            stage_kernel, numbers=numbers, spot_row=spot_row, n_refs=n_refs, final=final
        ),
        out_shape=out_shape,
        grid_spec=pltpu.PrefetchScalarGridSpec(
            num_scalar_prefetch=1,
            grid=(),
            in_specs=[whole] * 5,
            out_specs=[whole] * len(out_shape),
            scratch_shapes=[pltpu.VMEM((2, BLOCK, width), query.dtype)],
        ),
        input_output_aliases={4: len(out_shape) - 2, 5: len(out_shape) - 1},
        compiler_params=pltpu.CompilerParams(vmem_limit_bytes=40 * 1024 * 1024),
        cost_estimate=pl.CostEstimate(
            flops=4 * pairs * width,
            bytes_accessed=8 * acc.size,
            transcendentals=pairs * width // HEAD_DIM,
        ),
    )(plan, *received, query, acc, stat)


def shards(queries, keys, values, epi_dev, epi_frame, epi_block, valid, ref_local, *, n_tm, n_tok):
    inner = math.gcd(SPAN, max(1, HEADS // n_tok))
    n_outer = n_tm // inner
    n_ranks = inner * n_tok
    units = n_ranks * FRAMES_DEV
    width = keys.shape[2] // n_ranks
    rounds, room = n_outer - 1, -(-units * 5 // 8)
    ref_near = inner % SPAN == 0
    plane_groups = [
        [(o * inner + i) * n_tok + t for i in range(inner) for t in range(n_tok)]
        for o in range(n_outer)
    ]

    def exchange(x):
        return lax.all_to_all(
            x, ("tm", "tok"), 0, 0, axis_index_groups=plane_groups, tiled=True
        )

    def shift(x, way):
        pairs = [
            (o * inner + i, (o + way) * inner + i)
            for o in range(n_outer)
            for i in range(inner)
            if 0 <= o + way < n_outer
        ]
        return lax.ppermute(x, "tm", pairs)

    my_outer = (lax.axis_index("tm") // inner).astype(jnp.int32)
    plan = make_plan(
        epi_dev, epi_frame, epi_block, valid, ref_local, my_outer, inner, n_tok, rounds, room
    )
    three = jnp.stack([queries, keys, values]).reshape(3, FRAMES_DEV, BLOCK, n_ranks, width)
    own = exchange(three.transpose(3, 1, 0, 2, 4)).reshape(units, 3, BLOCK, width)
    n_local = inner * FRAMES_DEV
    n_refs = 0 if ref_near else n_tok

    def passed(own, spot_row, send):
        received = None
        for step in range(1, rounds + 1):
            arriving = [shift(sent, 2 * way - 1) for way, sent in enumerate(send(own, received, step))]
            if step == 1:
                query, acc, stat = near(plan, own, n_local, n_tok, spot_row, ref_near)
            else:
                numbers = (step - 1, rounds + step - 1)
                acc, stat = stage(
                    plan, received, query, acc, stat, numbers, n_ranks, spot_row, n_refs, False
                )
            own, acc = lax.optimization_barrier((own, acc))
            received = arriving
        numbers = (rounds, 2 * rounds)
        return stage(plan, received, query, acc, stat, numbers, n_ranks, spot_row, n_refs, True)[0]

    def listed(own):
        return passed(own, 3, lambda own, got, step: pack(plan, own, got or [], step, room))

    def gathered(own):
        return passed(own, 5, lambda own, got, step: got or [own[:, 1:3]] * 2)

    attended = exchange(lax.cond(plan[2, 0] <= rounds, listed, gathered, own))
    return attended.transpose(1, 2, 0, 3).reshape(queries.shape)


def solution(mesh):
    return jax.shard_map(
        functools.partial(shards, n_tm=mesh.shape["tm"], n_tok=mesh.shape["tok"]),
        mesh=mesh,
        in_specs=(P("tm", "tok", None),) * 3 + (P(),) * 5,
        out_specs=P("tm", "tok", None),
        check_vma=False,
    )
```

```python
import functools
import math

import jax
import jax.numpy as jnp
from jax import lax
from jax.experimental import pallas as pl
from jax.experimental.pallas import tpu as pltpu
from jax.sharding import PartitionSpec as P

HEADS = 16
HEAD_DIM = 64
BLOCK = 128
FRAMES_DEV = 2
ENTRIES = 6
SPAN = 4


def plan_kernel(
    me_ref, ref_ref, dev_hbm, place_hbm, block_hbm, valid_hbm, out_ref, entries, sems,
    *, inner, n_tok, rounds, rooms,
):
    copies = [
        pltpu.make_async_copy(array, entries.at[index], sems.at[index])
        for index, array in enumerate((dev_hbm, place_hbm, block_hbm, valid_hbm))
    ]
    for copy in copies:
        copy.start()
    for copy in copies:
        copy.wait()
    n_frames = dev_hbm.shape[0]
    units = inner * n_tok * FRAMES_DEV
    plane_frames = inner * FRAMES_DEV
    n_outer = n_frames // plane_frames
    lanes = out_ref.shape[1]
    f32 = jnp.float32
    me = me_ref[0].astype(f32)
    dev, place = entries[0], entries[1]
    ids = (dev // inner) * units + ((dev % inner) * n_tok + entries[2]) * FRAMES_DEV + place
    used = entries[3] > 0
    frame_lane = lax.broadcasted_iota(jnp.int32, (n_frames, lanes), 1)
    hit = jnp.zeros((n_frames, lanes), f32)
    for entry in range(ENTRIES):
        here = (ids[:, entry : entry + 1] == frame_lane) & used[:, entry : entry + 1]
        hit = jnp.where(here, 1.0, hit)
    lane = lax.broadcasted_iota(jnp.int32, (1, lanes), 1)
    unit = lane % units
    origin = (lane // units).astype(f32)
    need = []
    for plane in range(n_outer):
        rows = lax.slice_in_dim(hit, plane * plane_frames, (plane + 1) * plane_frames)
        wanted = jnp.max(rows, axis=0, keepdims=True) > 0
        if inner % SPAN:
            group = plane * inner // SPAN
            ref_frame = group * (SPAN * FRAMES_DEV) + ref_ref[group]
            ref_dev = ref_frame // FRAMES_DEV
            wanted = wanted | (
                (lane // (n_tok * FRAMES_DEV) == ref_dev)
                & (lane % FRAMES_DEV == ref_frame % FRAMES_DEV)
            )
        need.append(wanted)

    square_row = lax.broadcasted_iota(jnp.int32, (lanes, lanes), 0)
    square_lane = lax.broadcasted_iota(jnp.int32, (lanes, lanes), 1)
    diagonal = square_row == square_lane
    earlier = square_row < square_lane

    def column(row):
        return jnp.sum(jnp.where(diagonal, row, 0.0), axis=1, keepdims=True)

    def count(mask, axis):
        return jnp.sum(jnp.where(mask, 1.0, 0.0), axis=axis, keepdims=True)

    def ranking(start, reach):
        start_col, reach_col = column(start), column(reach)
        ahead = (reach_col > reach) | ((reach_col == reach) & earlier)
        return count((start_col == start) & (reach_col > 0) & ahead, 0)

    def departure(start, reach, rank, room):
        depart = jnp.zeros_like(start)
        for plane in range(n_outer - 1, 0, -1):
            total = jnp.zeros((1, 1), f32)
            turn = jnp.ones_like(start)
            for step in range(1, rounds + 1):
                if plane < n_outer - 1:
                    passing = (
                        (start > plane)
                        & (start - reach <= plane - 1)
                        & (depart + (start - plane) == step)
                        & (reach > 0)
                    )
                    total = total + (room - count(passing, 1))
                else:
                    total = total + room
                turn = turn + jnp.where(total <= rank, 1.0, 0.0)
            depart = jnp.where((start == plane) & (reach > 0), turn, depart)
        last = jnp.max(jnp.where(reach > 0, depart + reach - 1.0, 0.0), axis=1, keepdims=True)
        return depart, last

    def one_way(start, reach, here, depart):
        def on_link(link):
            crosses = (reach > 0) & (start > link) & (start - reach <= link)
            step = jnp.where(crosses, depart + (start - 1.0 - link), -1.0)
            slot = count((column(step) == step) & earlier, 0)
            return crosses, step, slot

        arrives, in_step, in_slot = on_link(here)
        leaves, out_step, out_slot = on_link(here - 1.0)
        source = jnp.where(start == here, unit.astype(f32), units + in_slot)
        key = column(jnp.where(leaves, (out_step - 1.0) * units + out_slot, -1.0))
        sent = jnp.sum(
            jnp.where(key == square_lane.astype(f32), column(source), 0.0), axis=0, keepdims=True
        )
        return arrives, in_step, in_slot, sent

    lowest, highest = origin, origin
    for plane in range(n_outer):
        highest = jnp.where(need[plane] & (origin < plane), float(plane), highest)
        other = n_outer - 1 - plane
        lowest = jnp.where(need[other] & (origin > other), float(other), lowest)
    top = n_outer - 1.0
    ways = [(origin, origin - lowest), (top - origin, highest - origin)]
    ranks = [ranking(*way) for way in ways]
    chosen = jnp.full((1, 1), float(len(rooms)), f32)
    departs = [jnp.zeros_like(origin)] * 2
    for index in reversed(range(len(rooms))):
        tried = [departure(*way, rank, rooms[index]) for way, rank in zip(ways, ranks)]
        fits = jnp.maximum(tried[0][1], tried[1][1]) <= rounds
        chosen = jnp.where(fits, float(index), chosen)
        departs = [jnp.where(fits, new[0], old) for new, old in zip(tried, departs)]
    down = one_way(*ways[0], me, departs[0])
    up = one_way(*ways[1], top - me, departs[1])
    unit_f = unit.astype(f32)
    spots = unit_f
    for way, (arrives, in_step, in_slot, _) in enumerate((down, up)):
        spots = jnp.where(arrives, (in_step + way * rounds) * 1024 + in_slot, spots)
    distance = origin - me
    full = jnp.where(distance > 0, distance, jnp.where(distance < 0, n_outer - 1 - distance, 0))
    full = full * 1024 + unit_f
    first = me * plane_frames
    row_frame = lax.broadcasted_iota(jnp.int32, (n_frames, lanes), 0).astype(f32)
    wide_lane = frame_lane.astype(f32)
    group = me_ref[0] * inner // SPAN
    ref_frame = group * (SPAN * FRAMES_DEV) + ref_ref[group]
    ref_dev = ref_frame // FRAMES_DEV

    def places(table):
        listed = jnp.zeros((1, lanes), f32)
        for entry in range(ENTRIES):
            mine, live = ids[:, entry : entry + 1], used[:, entry : entry + 1]
            found = jnp.sum(jnp.where(mine == frame_lane, table, 0.0), axis=1, keepdims=True)
            found = jnp.where(live, found, 65536.0)
            target = (row_frame - first) * 8 + entry
            listed += jnp.sum(jnp.where(target == wide_lane, found, 0.0), axis=0, keepdims=True)
        listed = jnp.where(lane % 8 < ENTRIES, listed, 65536.0)
        refs = jnp.zeros((1, lanes), f32)
        for block in range(n_tok):
            which = (ref_dev * n_tok + block) * FRAMES_DEV + ref_frame % FRAMES_DEV
            found = jnp.sum(jnp.where(lane == which, table, 0.0), axis=1, keepdims=True)
            refs = jnp.where(lane == block, found, refs)
        return [listed, refs]

    rows = [down[3], up[3], chosen + jnp.zeros_like(origin)] + places(spots) + places(full)
    for index, row in enumerate(rows):
        out_ref[index : index + 1, :] = row.astype(jnp.int32)


def make_plan(epi_dev, epi_frame, epi_block, valid, ref_local, my_outer, inner, n_tok, rounds, rooms):
    n_blocks = epi_dev.shape[0] * n_tok
    lanes = -(-n_blocks // 128) * 128
    smem, anywhere = pl.BlockSpec(memory_space=pltpu.SMEM), pl.BlockSpec(memory_space=pl.ANY)
    return pl.pallas_call(
        functools.partial(plan_kernel, inner=inner, n_tok=n_tok, rounds=rounds, rooms=rooms),
        out_shape=jax.ShapeDtypeStruct((8, lanes), jnp.int32),
        in_specs=[smem, smem] + [anywhere] * 4,
        out_specs=pl.BlockSpec(memory_space=pltpu.VMEM),
        scratch_shapes=[
            pltpu.VMEM((4,) + epi_dev.shape, jnp.int32),
            pltpu.SemaphoreType.DMA((4,)),
        ],
        compiler_params=pltpu.CompilerParams(vmem_limit_bytes=32 * 1024 * 1024),
    )(my_outer.reshape(1), ref_local, epi_dev, epi_frame, epi_block, valid)


def pack_kernel(plan_ref, *refs, step, room, units):
    sources, targets = refs[:-2], refs[-2:]
    own = sources[0]
    for way, target in enumerate(targets):
        for slot in range(room):
            code = plan_ref[way, (step - 1) * units + slot]
            if step == 1:
                target[slot] = own[code, 1:3]
            else:

                @pl.when(code < units)
                def _():
                    target[slot] = own[code, 1:3]

                @pl.when(code >= units)
                def _():
                    target[slot] = sources[1 + way][code - units]


def pack(plan, own, previous, step, room):
    out = jax.ShapeDtypeStruct((room, 2) + own.shape[2:], own.dtype)
    whole = pl.BlockSpec(memory_space=pltpu.VMEM)
    return pl.pallas_call(
        functools.partial(pack_kernel, step=step, room=room, units=own.shape[0]),
        out_shape=(out, out),
        grid_spec=pltpu.PrefetchScalarGridSpec(
            num_scalar_prefetch=1,
            grid=(),
            in_specs=[whole] * (1 + len(previous)),
            out_specs=(whole, whole),
        ),
        compiler_params=pltpu.CompilerParams(vmem_limit_bytes=24 * 1024 * 1024),
        cost_estimate=pl.CostEstimate(
            flops=0, bytes_accessed=8 * math.prod(out.shape), transcendentals=0
        ),
    )(plan, own, *previous)


def fold(keys, values, query, acc, stat, fresh):
    width, tile = acc.shape
    scores = jnp.dot(keys, query, preferred_element_type=jnp.float32)
    top = jnp.max(scores, axis=0, keepdims=True)
    if not fresh:
        old_top = stat[0:1]
        top = jnp.maximum(old_top, top)
    weights = jnp.exp(scores - top)
    total = jnp.sum(weights, axis=0, keepdims=True)
    weights = weights.astype(jnp.bfloat16)
    if not fresh:
        keep = jnp.exp(old_top - top)
        total = stat[1:2] * keep + total
    stat[0:1] = top
    stat[1:2] = total
    channels = values.T
    for head in range(width // HEAD_DIM):
        rows, lanes = pl.ds(head * HEAD_DIM, HEAD_DIM), slice(head * tile, (head + 1) * tile)
        attended = jnp.dot(
            channels[head * HEAD_DIM : (head + 1) * HEAD_DIM],
            weights[:, lanes],
            preferred_element_type=jnp.float32,
        )
        acc[rows] = attended if fresh else acc[rows] * keep[:, lanes] + attended


def listed_items(plan_ref, sources, block_set, query_ref, acc_ref, stat_ref, spot_row, n_refs):
    n_local, n_tiles = acc_ref.shape[:2]

    def item(local, code):
        spot, origin = code & 1023, code >> 10
        for number, (source, first) in sources.items():

            @pl.when(origin == number)
            def _():
                block_set[...] = source[spot, first : first + 2]

        hit = functools.reduce(jnp.logical_or, [origin == number for number in sources])

        @pl.when(hit)
        def _():
            for tile in range(n_tiles):
                fold(
                    block_set[0], block_set[1], query_ref[local, tile], acc_ref.at[local, tile],
                    stat_ref.at[local, tile], False,
                )

    @pl.loop(0, n_local * 8)
    def _(index):
        item(index >> 3, plan_ref[spot_row, index])

    if n_refs:

        @pl.loop(0, n_local * n_refs)
        def _(index):
            item(lax.div(index, n_refs), plan_ref[spot_row + 1, lax.rem(index, n_refs)])


def near_kernel(plan_ref, own_ref, query_ref, acc_ref, stat_ref, *, n_tok, spot_row, ref_near):
    n_local, n_tiles, width, tile = acc_ref.shape
    heads = width // HEAD_DIM
    row_head = lax.broadcasted_iota(jnp.int32, (width, 1), 0) // HEAD_DIM

    @pl.loop(0, n_local, unroll=math.gcd(4, n_local))
    def _(local):
        base = (local // FRAMES_DEV) * (n_tok * FRAMES_DEV) + local % FRAMES_DEV
        spots = [base + block * FRAMES_DEV for block in range(n_tok)]
        blocks = [own_ref.at[spot] for spot in spots]
        if ref_near:
            blocks += [own_ref.at[plan_ref[spot_row + 1, block]] for block in range(n_tok)]
        keys = jnp.concatenate([block[1] for block in blocks], 0)
        values = jnp.concatenate([block[2] for block in blocks], 0)
        for index in range(n_tiles):
            first = index * tile // BLOCK
            turned = jnp.concatenate(
                [own_ref[spot, 0].T for spot in spots[first : first + tile // BLOCK]], 1
            )
            turned = turned * jnp.asarray(HEAD_DIM**-0.5, turned.dtype)
            query = jnp.concatenate(
                [jnp.where(row_head == head, turned, jnp.zeros_like(turned)) for head in range(heads)],
                1,
            )
            query_ref[local, index] = query
            fold(keys, values, query, acc_ref.at[local, index], stat_ref.at[local, index], True)


def near(plan, own, n_local, n_tok, spot_row, ref_near):
    width = own.shape[-1]
    rows = n_tok * BLOCK
    tile = math.gcd(rows, 256)
    lanes = tile * (width // HEAD_DIM)
    whole = pl.BlockSpec(memory_space=pltpu.VMEM)
    pairs = n_local * rows * (1 + ref_near) * rows
    return pl.pallas_call(
        functools.partial(near_kernel, n_tok=n_tok, spot_row=spot_row, ref_near=ref_near),
        out_shape=(
            jax.ShapeDtypeStruct((n_local, rows // tile, width, lanes), own.dtype),
            jax.ShapeDtypeStruct((n_local, rows // tile, width, tile), jnp.float32),
            jax.ShapeDtypeStruct((n_local, rows // tile, 2, lanes), jnp.float32),
        ),
        grid_spec=pltpu.PrefetchScalarGridSpec(
            num_scalar_prefetch=1,
            grid=(),
            in_specs=[whole],
            out_specs=(whole, whole, whole),
        ),
        compiler_params=pltpu.CompilerParams(vmem_limit_bytes=40 * 1024 * 1024),
        cost_estimate=pl.CostEstimate(
            flops=4 * pairs * width,
            bytes_accessed=16 * n_local * rows * width,
            transcendentals=pairs * width // HEAD_DIM,
        ),
    )(plan, own)


def stage_kernel(
    plan_ref, query_ref, acc_in, stat_in, *refs, numbers, spot_row, n_refs, final
):
    acc_ref, stat_ref, block_set = refs[-3:]
    sources = {n: (ref, 0 if n else 1) for n, ref in zip(numbers, refs)}
    if final:
        out_ref = refs[-4]
    listed_items(plan_ref, sources, block_set, query_ref, acc_ref, stat_ref, spot_row, n_refs)
    if not final:
        return
    n_local, n_tiles, width, tile = acc_ref.shape
    n_tok = n_tiles * tile // BLOCK
    row_head = lax.broadcasted_iota(jnp.int32, (width, 1), 0) // HEAD_DIM

    @pl.loop(0, n_local, unroll=math.gcd(4, n_local))
    def _(local):
        for index in range(n_tiles):
            total = stat_ref[local, index][1:2]
            share = 1.0 / total[:, :tile]
            for head in range(1, width // HEAD_DIM):
                other = 1.0 / total[:, head * tile : (head + 1) * tile]
                share = jnp.where(row_head == head, other, share)
            result = (acc_ref[local, index] * share).astype(out_ref.dtype).T
            for block in range(tile // BLOCK):
                rank = (local // FRAMES_DEV) * n_tok + index * (tile // BLOCK) + block
                out_ref[rank, local % FRAMES_DEV] = result[block * BLOCK : (block + 1) * BLOCK]


def stage(plan, received, query, acc, stat, numbers, n_ranks, spot_row, n_refs, final):
    width = acc.shape[2]
    whole = pl.BlockSpec(memory_space=pltpu.VMEM)
    out_shape = [jax.ShapeDtypeStruct(x.shape, x.dtype) for x in (acc, stat)]
    if final:
        out_shape = [
            jax.ShapeDtypeStruct((n_ranks, FRAMES_DEV, BLOCK, width), query.dtype)
        ] + out_shape
    pairs = 2 * acc.size // width * BLOCK
    return pl.pallas_call(
        functools.partial(
            stage_kernel, numbers=numbers, spot_row=spot_row, n_refs=n_refs, final=final
        ),
        out_shape=out_shape,
        grid_spec=pltpu.PrefetchScalarGridSpec(
            num_scalar_prefetch=1,
            grid=(),
            in_specs=[whole] * (3 + len(received)),
            out_specs=[whole] * len(out_shape),
            scratch_shapes=[pltpu.VMEM((2, BLOCK, width), query.dtype)],
        ),
        input_output_aliases={2: len(out_shape) - 2, 3: len(out_shape) - 1},
        compiler_params=pltpu.CompilerParams(vmem_limit_bytes=40 * 1024 * 1024),
        cost_estimate=pl.CostEstimate(
            flops=4 * pairs * width,
            bytes_accessed=8 * acc.size,
            transcendentals=pairs * width // HEAD_DIM,
        ),
    )(plan, query, acc, stat, *received)


def shards(queries, keys, values, epi_dev, epi_frame, epi_block, valid, ref_local, *, n_tm, n_tok):
    inner = math.gcd(SPAN, max(1, HEADS // n_tok))
    n_outer = n_tm // inner
    n_ranks = inner * n_tok
    units = n_ranks * FRAMES_DEV
    width = keys.shape[2] // n_ranks
    rounds = n_outer - 1
    shares = (8, 9, 10, 12) if n_outer <= SPAN else (10,)
    rooms = [-(-units * share // 16) for share in shares]
    ref_near = inner % SPAN == 0
    plane_groups = [
        [(o * inner + i) * n_tok + t for i in range(inner) for t in range(n_tok)]
        for o in range(n_outer)
    ]

    def exchange(x):
        return lax.all_to_all(
            x, ("tm", "tok"), 0, 0, axis_index_groups=plane_groups, tiled=True
        )

    def shift(x, way):
        pairs = [
            (o * inner + i, (o + way) * inner + i)
            for o in range(n_outer)
            for i in range(inner)
            if 0 <= o + way < n_outer
        ]
        return lax.ppermute(x, "tm", pairs)

    my_outer = (lax.axis_index("tm") // inner).astype(jnp.int32)
    plan = make_plan(
        epi_dev, epi_frame, epi_block, valid, ref_local, my_outer, inner, n_tok, rounds, rooms
    )
    three = jnp.stack([queries, keys, values]).reshape(3, FRAMES_DEV, BLOCK, n_ranks, width)
    own = exchange(three.transpose(3, 1, 0, 2, 4)).reshape(units, 3, BLOCK, width)
    n_local = inner * FRAMES_DEV
    n_refs = 0 if ref_near else n_tok

    def passed(own, spot_row, send):
        received = None
        for step in range(1, rounds + 1):
            arriving = [shift(sent, 2 * way - 1) for way, sent in enumerate(send(own, received, step))]
            if step == 1:
                query, acc, stat = near(plan, own, n_local, n_tok, spot_row, ref_near)
            else:
                numbers = (step - 1, rounds + step - 1)
                if step == 2:
                    received, numbers = received + [own], numbers + (0,)
                acc, stat = stage(
                    plan, received, query, acc, stat, numbers, n_ranks, spot_row, n_refs, False
                )
            own, acc = lax.optimization_barrier((own, acc))
            received = arriving
        numbers = (rounds, 2 * rounds)
        return stage(plan, received, query, acc, stat, numbers, n_ranks, spot_row, n_refs, True)[0]

    def listed(room):
        return lambda own: passed(
            own, 3, lambda own, got, step: pack(plan, own, got or [], step, room)
        )

    def gathered(own):
        return passed(own, 5, lambda own, got, step: got or [own[:, 1:3]] * 2)

    attended = exchange(
        lax.switch(plan[2, 0], [listed(room) for room in rooms] + [gathered], own)
    )
    return attended.transpose(1, 2, 0, 3).reshape(queries.shape)


def solution(mesh):
    return jax.shard_map(
        functools.partial(shards, n_tm=mesh.shape["tm"], n_tok=mesh.shape["tok"]),
        mesh=mesh,
        in_specs=(P("tm", "tok", None),) * 3 + (P(),) * 5,
        out_specs=P("tm", "tok", None),
        check_vma=False,
    )
```

```python
import functools
import math

import jax
import jax.numpy as jnp
from jax import lax
from jax.experimental import pallas as pl
from jax.experimental.pallas import tpu as pltpu
from jax.sharding import PartitionSpec as P

HEADS = 16
HEAD_DIM = 64
BLOCK = 128
FRAMES_DEV = 2
ENTRIES = 6
SPAN = 4
FAR = 1024
DEAD = 65536
BATCH = 4

STRIDE = FRAMES_DEV + 1
WHOLE = pl.BlockSpec(memory_space=pltpu.VMEM)


def split_kernel(q_hbm, k_hbm, v_hbm, out_ref, q_ref, k_ref, v_ref, sems):
    copies = [
        pltpu.make_async_copy(source, target, sems.at[index])
        for index, (source, target) in enumerate(
            ((q_hbm, q_ref), (k_hbm, k_ref), (v_hbm, v_ref))
        )
    ]
    for copy in copies:
        copy.start()
    for copy in copies:
        copy.wait()
    for rank in range(out_ref.shape[0]):
        lanes = slice(rank * HEAD_DIM, (rank + 1) * HEAD_DIM)
        for frame in range(FRAMES_DEV):
            out_ref[rank, frame] = jnp.concatenate(
                [k_ref[frame, :, lanes], v_ref[frame, :, lanes]], 1
            )
        out_ref[rank, FRAMES_DEV] = jnp.concatenate(
            [q_ref[frame, :, lanes] for frame in range(FRAMES_DEV)], 1
        )


def merge_kernel(x_ref, out_ref):
    for frame in range(FRAMES_DEV):
        part = slice(frame * HEAD_DIM, (frame + 1) * HEAD_DIM)
        for rank in range(0, x_ref.shape[0], 2):
            out_ref[frame, :, rank * HEAD_DIM : (rank + 2) * HEAD_DIM] = jnp.concatenate(
                [x_ref[rank, :, part], x_ref[rank + 1, :, part]], 1
            )


def plan_kernel(
    me_ref, ref_ref, dev_hbm, place_hbm, block_hbm, valid_hbm, out_ref, entries, sems,
    *, inner, n_tok, rooms,
):
    copies = [
        pltpu.make_async_copy(array, entries.at[index], sems.at[index])
        for index, array in enumerate((dev_hbm, place_hbm, block_hbm, valid_hbm))
    ]
    for copy in copies:
        copy.start()
    for copy in copies:
        copy.wait()
    n_frames = dev_hbm.shape[0]
    units = inner * n_tok * STRIDE
    group_frames = inner * FRAMES_DEV
    n_outer = n_frames // group_frames
    lanes = out_ref.shape[1]
    f32 = jnp.float32
    me = me_ref[0].astype(f32)
    dev = entries[0]
    ids = (dev // inner) * units + ((dev % inner) * n_tok + entries[2]) * STRIDE + entries[1]
    used = entries[3] > 0
    frame_lane = lax.broadcasted_iota(jnp.int32, (n_frames, lanes), 1)
    hit = jnp.zeros((n_frames, lanes), f32)
    for entry in range(ENTRIES):
        here = (ids[:, entry : entry + 1] == frame_lane) & used[:, entry : entry + 1]
        hit = jnp.where(here, 1.0, hit)
    lane = lax.broadcasted_iota(jnp.int32, (1, lanes), 1)
    unit = (lane % units).astype(f32)
    origin = (lane // units).astype(f32)
    crosses = jnp.zeros((1, lanes), f32)
    for group in range(n_outer):
        rows = lax.slice_in_dim(hit, group * group_frames, (group + 1) * group_frames)
        wanted = jnp.max(rows, axis=0, keepdims=True)
        crosses = jnp.where(origin != group, jnp.maximum(wanted, crosses), crosses)

    def count(mask, axis):
        return jnp.sum(jnp.where(mask, 1.0, 0.0), axis=axis, keepdims=True)

    steps = jnp.where(origin > me, me - origin + n_outer, me - origin)
    everything = jnp.where(origin == me, unit, FAR + (steps - 1.0) * units + unit)
    sent, spots, chosen = jnp.zeros_like(origin), everything, jnp.full((1, 1), float(len(rooms)), f32)
    if rooms:
        square_row = lax.broadcasted_iota(jnp.int32, (lanes, lanes), 0)
        square_lane = lax.broadcasted_iota(jnp.int32, (lanes, lanes), 1)

        def column(row):
            return jnp.sum(jnp.where(square_row == square_lane, row, 0.0), axis=1, keepdims=True)

        key = jnp.where(crosses > 0, origin, -1.0)
        slot = count((column(key) == key) & (square_row < square_lane), 0)
        most = jnp.max(jnp.where(crosses > 0, slot + 1.0, 0.0), axis=1, keepdims=True)
        for index in reversed(range(len(rooms))):
            chosen = jnp.where(most <= rooms[index], float(index), chosen)
        mine = column(jnp.where((crosses > 0) & (origin == me), slot, -1.0))
        sent = jnp.sum(
            jnp.where(mine == square_lane.astype(f32), column(unit), 0.0), axis=0, keepdims=True
        )
        spots = jnp.where(origin == me, unit, FAR + slot)

    row_frame = lax.broadcasted_iota(jnp.int32, (n_frames, lanes), 0).astype(f32)
    wide_lane = frame_lane.astype(f32)

    def places(table):
        listed = jnp.zeros((1, lanes), f32)
        for entry in range(ENTRIES):
            mine, live = ids[:, entry : entry + 1], used[:, entry : entry + 1]
            found = jnp.sum(jnp.where(mine == frame_lane, table, 0.0), axis=1, keepdims=True)
            found = jnp.where(live, found, float(DEAD))
            target = (row_frame - me * group_frames) * 8 + entry
            listed += jnp.sum(jnp.where(target == wide_lane, found, 0.0), axis=0, keepdims=True)
        listed = jnp.where(lane % 8 < ENTRIES, listed, float(DEAD))
        refs = jnp.zeros((1, lanes), f32)
        for local in range(max(1, inner // SPAN)):
            scene = me_ref[0] * inner // SPAN + local
            ref_frame = scene * (SPAN * FRAMES_DEV) + ref_ref[scene]
            ref_dev = ref_frame // FRAMES_DEV
            base = (ref_dev // inner) * units + (ref_dev % inner) * n_tok * STRIDE
            for block in range(n_tok):
                which = base + block * STRIDE + ref_frame % FRAMES_DEV
                found = jnp.sum(jnp.where(lane == which, table, 0.0), axis=1, keepdims=True)
                refs = jnp.where(lane == local * n_tok + block, found, refs)
        return [listed, refs]

    rows = [sent, chosen + jnp.zeros_like(origin)] + places(spots) + places(everything)
    for index, row in enumerate(rows):
        out_ref[index : index + 1, :] = row.astype(jnp.int32)


def make_plan(epi_dev, epi_frame, epi_block, valid, ref_local, my_outer, inner, n_tok, rooms):
    n_outer = epi_dev.shape[0] // (inner * FRAMES_DEV)
    n_units = n_outer * inner * n_tok * STRIDE
    lanes = -(-n_units // 128) * 128
    smem, anywhere = pl.BlockSpec(memory_space=pltpu.SMEM), pl.BlockSpec(memory_space=pl.ANY)
    return pl.pallas_call(
        functools.partial(plan_kernel, inner=inner, n_tok=n_tok, rooms=rooms),
        out_shape=jax.ShapeDtypeStruct((8, lanes), jnp.int32),
        in_specs=[smem, smem] + [anywhere] * 4,
        out_specs=WHOLE,
        scratch_shapes=[
            pltpu.VMEM((4,) + epi_dev.shape, jnp.int32),
            pltpu.SemaphoreType.DMA((4,)),
        ],
        compiler_params=pltpu.CompilerParams(vmem_limit_bytes=32 * 1024 * 1024),
    )(my_outer.reshape(1), ref_local, epi_dev, epi_frame, epi_block, valid)


def pack_kernel(plan_ref, own_ref, *targets):
    first = 0
    for target in targets:
        for slot in range(target.shape[0]):
            target[slot] = own_ref[plan_ref[0, first + slot]]
        first += target.shape[0]


def pack(plan, own, sizes):
    return pl.pallas_call(
        pack_kernel,
        out_shape=[jax.ShapeDtypeStruct((size,) + own.shape[1:], own.dtype) for size in sizes],
        grid_spec=pltpu.PrefetchScalarGridSpec(
            num_scalar_prefetch=1,
            grid=(),
            in_specs=[WHOLE],
            out_specs=[WHOLE] * len(sizes),
        ),
        compiler_params=pltpu.CompilerParams(vmem_limit_bytes=24 * 1024 * 1024),
        cost_estimate=pl.CostEstimate(
            flops=0, bytes_accessed=4 * sum(sizes) * own[0].size, transcendentals=0
        ),
    )(plan, own)


def part_of(pairs, query):
    scores = jnp.dot(pairs, query, preferred_element_type=jnp.float32)
    top = jnp.max(scores, axis=0, keepdims=True)
    weights = jnp.exp(scores - top)
    total = jnp.sum(weights, axis=0, keepdims=True)
    attended = jnp.dot(
        pairs.T[HEAD_DIM:], weights.astype(jnp.bfloat16), preferred_element_type=jnp.float32
    )
    return attended, top, total


def near_kernel(plan_ref, own_ref, query_ref, acc_ref, stat_ref, *, n_tok, spot_row, ref_near):
    n_local, n_tiles, _, tile = acc_ref.shape
    inner = n_local // FRAMES_DEV

    @pl.loop(0, inner, unroll=math.gcd(2, inner))
    def _(chip):
        spots = [(chip * n_tok + block) * STRIDE for block in range(n_tok)]
        refs = []
        if ref_near:
            scene = chip // SPAN * n_tok
            refs = [own_ref[plan_ref[spot_row + 1, scene + block]] for block in range(n_tok)]
        turned = [own_ref[spot + FRAMES_DEV].T for spot in spots]
        for frame in range(FRAMES_DEV):
            pairs = jnp.concatenate([own_ref[spot + frame] for spot in spots] + refs, 0)
            local = chip * FRAMES_DEV + frame
            for index in range(n_tiles):
                first = index * tile // BLOCK
                query = jnp.concatenate(
                    [
                        block[frame * HEAD_DIM : (frame + 1) * HEAD_DIM]
                        for block in turned[first : first + tile // BLOCK]
                    ],
                    1,
                ) * jnp.asarray(HEAD_DIM**-0.5, own_ref.dtype)
                query = jnp.concatenate([query, jnp.zeros_like(query)], 0)
                query_ref[local, index] = query
                attended, top, total = part_of(pairs, query)
                acc_ref[local, index] = attended
                stat_ref[local, index, 0:1] = top
                stat_ref[local, index, 1:2] = total


def near(plan, own, inner, n_tok, spot_row, ref_near):
    rows = n_tok * BLOCK
    tile = math.gcd(rows, 256)
    n_local = inner * FRAMES_DEV
    pairs = n_local * rows * (1 + ref_near) * rows
    lead = (n_local, rows // tile)
    return pl.pallas_call(
        functools.partial(near_kernel, n_tok=n_tok, spot_row=spot_row, ref_near=ref_near),
        out_shape=(
            jax.ShapeDtypeStruct(lead + (2 * HEAD_DIM, tile), own.dtype),
            jax.ShapeDtypeStruct(lead + (HEAD_DIM, tile), jnp.float32),
            jax.ShapeDtypeStruct(lead + (2, tile), jnp.float32),
        ),
        grid_spec=pltpu.PrefetchScalarGridSpec(
            num_scalar_prefetch=1,
            grid=(),
            in_specs=[WHOLE],
            out_specs=(WHOLE, WHOLE, WHOLE),
        ),
        compiler_params=pltpu.CompilerParams(vmem_limit_bytes=40 * 1024 * 1024),
        cost_estimate=pl.CostEstimate(
            flops=8 * pairs * HEAD_DIM,
            bytes_accessed=16 * n_local * rows * HEAD_DIM,
            transcendentals=pairs,
        ),
    )(plan, own)


def stage_kernel(
    plan_ref, query_ref, acc_in, stat_in, source_ref, *refs, low, high, spot_row, n_refs, final
):
    acc_ref, stat_ref, items = refs[-3:]
    n_local, n_tiles, _, tile = acc_ref.shape

    def list_up(row, per_frame):
        def one(index, found):
            code = plan_ref[row, lax.rem(index, per_frame) if row > spot_row else index]
            items[found] = lax.div(index, per_frame) * DEAD + (code - low)
            return found + ((code >= low) & (code < high)).astype(jnp.int32)

        return one

    found = lax.fori_loop(0, n_local * 8, list_up(spot_row, 8), jnp.int32(0), unroll=8)
    if n_refs:
        found = lax.fori_loop(0, n_local * n_refs, list_up(spot_row + 1, n_refs), found)

    @pl.loop(0, lax.div(found + (BATCH - 1), jnp.int32(BATCH)))
    def _(step):
        for index in range(n_tiles):
            parts = []
            for turn in range(BATCH):
                here = step * BATCH + turn < found
                word = items[jnp.where(here, step * BATCH + turn, 0)]
                local = word >> 16
                parts.append((here, local, part_of(source_ref[word & (DEAD - 1)], query_ref[local, index])))
            for here, local, (attended, top, total) in parts:
                old_top = stat_ref[local, index, 0:1]
                new_top = jnp.where(here, jnp.maximum(old_top, top), old_top)
                keep = jnp.exp(old_top - new_top)
                add = jnp.where(here, jnp.exp(jnp.minimum(top - new_top, 0.0)), 0.0)
                acc_ref[local, index] = acc_ref[local, index] * keep + attended * add
                stat_ref[local, index, 1:2] = stat_ref[local, index, 1:2] * keep + total * add
                stat_ref[local, index, 0:1] = new_top

    if not final:
        return
    out_ref = refs[0]
    n_tok = n_tiles * tile // BLOCK
    inner = n_local // FRAMES_DEV

    @pl.loop(0, inner, unroll=math.gcd(4, inner))
    def _(chip):
        for index in range(n_tiles):
            parts = []
            for frame in range(FRAMES_DEV):
                local = chip * FRAMES_DEV + frame
                parts.append(acc_ref[local, index] * (1.0 / stat_ref[local, index][1:2]))
            result = jnp.concatenate(parts, 0).astype(out_ref.dtype).T
            for block in range(tile // BLOCK):
                out_ref[chip * n_tok + index * (tile // BLOCK) + block] = result[
                    block * BLOCK : (block + 1) * BLOCK
                ]


def stage(plan, source, query, acc, stat, low, n_ranks, spot_row, n_refs, final):
    out_shape = [jax.ShapeDtypeStruct(x.shape, x.dtype) for x in (acc, stat)]
    if final:
        result = jax.ShapeDtypeStruct((n_ranks, BLOCK, FRAMES_DEV * HEAD_DIM), query.dtype)
        out_shape = [result] + out_shape
    pairs = 2 * acc.size // HEAD_DIM * BLOCK
    return pl.pallas_call(
        functools.partial(
            stage_kernel, low=low, high=low + source.shape[0], spot_row=spot_row,
            n_refs=n_refs, final=final,
        ),
        out_shape=out_shape,
        grid_spec=pltpu.PrefetchScalarGridSpec(
            num_scalar_prefetch=1,
            grid=(),
            in_specs=[WHOLE] * 4,
            out_specs=[WHOLE] * len(out_shape),
            scratch_shapes=[pltpu.SMEM((acc.shape[0] * (8 + n_refs) + 1,), jnp.int32)],
        ),
        input_output_aliases={2: len(out_shape) - 2, 3: len(out_shape) - 1},
        compiler_params=pltpu.CompilerParams(vmem_limit_bytes=40 * 1024 * 1024),
        cost_estimate=pl.CostEstimate(
            flops=8 * pairs * HEAD_DIM, bytes_accessed=8 * acc.size, transcendentals=pairs
        ),
    )(plan, query, acc, stat, source)


def shards(queries, keys, values, epi_dev, epi_frame, epi_block, valid, ref_local, *, n_tm, n_tok):
    inner = HEADS // n_tok
    n_outer = n_tm // inner
    n_ranks = inner * n_tok
    units = n_ranks * STRIDE
    ref_near = inner % SPAN == 0
    n_refs = 0 if ref_near else n_tok
    blocks = n_ranks * FRAMES_DEV
    rooms = [-(-blocks * share // 16) for share in (10, 11, 12, 13, 14)] if n_outer == 2 else []
    groups = [
        [(o * inner + i) * n_tok + t for i in range(inner) for t in range(n_tok)]
        for o in range(n_outer)
    ]

    def exchange(x):
        return lax.all_to_all(x, ("tm", "tok"), 0, 0, axis_index_groups=groups, tiled=True)

    def turn(x):
        return lax.ppermute(x, "tm", [(d, (d + inner) % n_tm) for d in range(n_tm)])

    my_outer = (lax.axis_index("tm") // inner).astype(jnp.int32)
    plan = make_plan(
        epi_dev, epi_frame, epi_block, valid, ref_local, my_outer, inner, n_tok, rooms
    )
    small = pltpu.CompilerParams(vmem_limit_bytes=24 * 1024 * 1024)
    own = pl.pallas_call(
        split_kernel,
        out_shape=jax.ShapeDtypeStruct((n_ranks, STRIDE, BLOCK, 2 * HEAD_DIM), keys.dtype),
        in_specs=[pl.BlockSpec(memory_space=pltpu.HBM)] * 3,
        out_specs=WHOLE,
        scratch_shapes=[pltpu.VMEM(keys.shape, keys.dtype)] * 3 + [pltpu.SemaphoreType.DMA((3,))],
        compiler_params=small,
    )(queries, keys, values)
    own = exchange(own).reshape(units, BLOCK, 2 * HEAD_DIM)

    def attend(own, arrivals, spot_row, waiting=None):
        query, acc, stat = near(plan, own, inner, n_tok, spot_row, ref_near)
        acc, stat = stage(plan, own, query, acc, stat, 0, n_ranks, spot_row, n_refs, False)
        if waiting is not None:
            waiting, acc = lax.optimization_barrier((waiting, acc))
            arrivals = arrivals + [turn(waiting)]
        low = FAR
        for index, arrived in enumerate(arrivals):
            final = index == len(arrivals) - 1
            *result, acc, stat = stage(
                plan, arrived, query, acc, stat, low, n_ranks, spot_row, n_refs, final
            )
            low += arrived.shape[0]
        return result[0]

    def listed(room):
        first = -(-room * 2 // 3)

        def run(own):
            early, late = pack(plan, own, (first, room - first))
            return attend(own, [turn(early)], 2, late)

        return run

    def gathered(own):
        arrivals = [turn(own)]
        for _ in range(n_outer - 2):
            arrivals.append(turn(arrivals[-1]))
        return attend(own, arrivals, 4)

    options = [listed(room) for room in rooms] + [gathered]
    attended = exchange(lax.switch(plan[1, 0], options, own))
    return pl.pallas_call(
        merge_kernel,
        out_shape=jax.ShapeDtypeStruct(queries.shape, queries.dtype),
        in_specs=[WHOLE],
        out_specs=WHOLE,
        compiler_params=small,
    )(attended)


def solution(mesh):
    return jax.shard_map(
        functools.partial(shards, n_tm=mesh.shape["tm"], n_tok=mesh.shape["tok"]),
        mesh=mesh,
        in_specs=(P("tm", "tok", None),) * 3 + (P(),) * 5,
        out_specs=P("tm", "tok", None),
        check_vma=False,
    )
```

```python
import functools
import math

import jax
import jax.numpy as jnp
from jax import lax
from jax.experimental import pallas as pl
from jax.experimental.pallas import tpu as pltpu
from jax.sharding import PartitionSpec as P

HEADS = 16
HEAD_DIM = 64
BLOCK = 128
FRAMES_DEV = 2
ENTRIES = 6
SPAN = 4
FAR = 1024
DEAD = 65536
BATCH_BITS = 2
BATCH = 1 << BATCH_BITS

STRIDE = FRAMES_DEV + 1
WHOLE = pl.BlockSpec(memory_space=pltpu.VMEM)


def split_kernel(q_hbm, k_hbm, v_hbm, out_ref, q_ref, k_ref, v_ref, sems):
    copies = [
        pltpu.make_async_copy(source, target, sems.at[index])
        for index, (source, target) in enumerate(
            ((q_hbm, q_ref), (k_hbm, k_ref), (v_hbm, v_ref))
        )
    ]
    for copy in copies:
        copy.start()
    for copy in copies:
        copy.wait()
    for rank in range(out_ref.shape[0]):
        lanes = slice(rank * HEAD_DIM, (rank + 1) * HEAD_DIM)
        for frame in range(FRAMES_DEV):
            out_ref[rank, frame] = jnp.concatenate(
                [k_ref[frame, :, lanes], v_ref[frame, :, lanes]], 1
            )
        out_ref[rank, FRAMES_DEV] = jnp.concatenate(
            [q_ref[frame, :, lanes] for frame in range(FRAMES_DEV)], 1
        )


def merge_kernel(x_ref, out_ref):
    for frame in range(FRAMES_DEV):
        part = slice(frame * HEAD_DIM, (frame + 1) * HEAD_DIM)
        for rank in range(0, x_ref.shape[0], 2):
            out_ref[frame, :, rank * HEAD_DIM : (rank + 2) * HEAD_DIM] = jnp.concatenate(
                [x_ref[rank, :, part], x_ref[rank + 1, :, part]], 1
            )


def plan_kernel(
    me_ref, ref_ref, dev_hbm, place_hbm, block_hbm, valid_hbm, out_ref, entries, sems,
    *, inner, n_tok, flip, rooms,
):
    copies = [
        pltpu.make_async_copy(array, entries.at[index], sems.at[index])
        for index, array in enumerate((dev_hbm, place_hbm, block_hbm, valid_hbm))
    ]
    for copy in copies:
        copy.start()
    for copy in copies:
        copy.wait()
    n_frames = dev_hbm.shape[0]
    units = inner * n_tok * STRIDE
    group_frames = inner * FRAMES_DEV
    n_outer = n_frames // group_frames
    lanes = out_ref.shape[1]
    f32 = jnp.float32
    me = me_ref[0].astype(f32)
    dev = entries[0]
    spot = (dev % inner + flip * (dev // inner)) % inner
    ids = (dev // inner) * units + (spot * n_tok + entries[2]) * STRIDE + entries[1]
    used = entries[3] > 0
    frame_lane = lax.broadcasted_iota(jnp.int32, (n_frames, lanes), 1)
    hit = jnp.zeros((n_frames, lanes), f32)
    for entry in range(ENTRIES):
        here = (ids[:, entry : entry + 1] == frame_lane) & used[:, entry : entry + 1]
        hit = jnp.where(here, 1.0, hit)
    lane = lax.broadcasted_iota(jnp.int32, (1, lanes), 1)
    unit = (lane % units).astype(f32)
    origin = (lane // units).astype(f32)
    crosses = jnp.zeros((1, lanes), f32)
    for group in range(n_outer):
        rows = lax.slice_in_dim(hit, group * group_frames, (group + 1) * group_frames)
        wanted = jnp.max(rows, axis=0, keepdims=True)
        crosses = jnp.where(origin != group, jnp.maximum(wanted, crosses), crosses)

    def count(mask, axis):
        return jnp.sum(jnp.where(mask, 1.0, 0.0), axis=axis, keepdims=True)

    steps = jnp.where(origin > me, me - origin + n_outer, me - origin)
    everything = jnp.where(origin == me, unit, FAR + (steps - 1.0) * units + unit)
    sent, spots, chosen = jnp.zeros_like(origin), everything, jnp.full((1, 1), float(len(rooms)), f32)
    if rooms:
        square_row = lax.broadcasted_iota(jnp.int32, (lanes, lanes), 0)
        square_lane = lax.broadcasted_iota(jnp.int32, (lanes, lanes), 1)

        def column(row):
            return jnp.sum(jnp.where(square_row == square_lane, row, 0.0), axis=1, keepdims=True)

        key = jnp.where(crosses > 0, origin, -1.0)
        slot = count((column(key) == key) & (square_row < square_lane), 0)
        most = jnp.max(jnp.where(crosses > 0, slot + 1.0, 0.0), axis=1, keepdims=True)
        for index in reversed(range(len(rooms))):
            chosen = jnp.where(most <= rooms[index], float(index), chosen)
        mine = column(jnp.where((crosses > 0) & (origin == me), slot, -1.0))
        sent = jnp.sum(
            jnp.where(mine == square_lane.astype(f32), column(unit), 0.0), axis=0, keepdims=True
        )
        spots = jnp.where(origin == me, unit, FAR + slot)

    row_frame = lax.broadcasted_iota(jnp.int32, (n_frames, lanes), 0).astype(f32)
    wide_lane = frame_lane.astype(f32)
    local_row = row_frame - me * group_frames
    turned = local_row + me * (flip * FRAMES_DEV)
    turned = jnp.where(turned >= group_frames, turned - group_frames, turned) * 8
    turned = jnp.where((local_row >= 0) & (local_row < group_frames), turned, -8.0)

    def places(table):
        listed = jnp.zeros((1, lanes), f32)
        for entry in range(ENTRIES):
            mine, live = ids[:, entry : entry + 1], used[:, entry : entry + 1]
            found = jnp.sum(jnp.where(mine == frame_lane, table, 0.0), axis=1, keepdims=True)
            found = jnp.where(live, found, float(DEAD))
            target = turned + entry
            listed += jnp.sum(jnp.where(target == wide_lane, found, 0.0), axis=0, keepdims=True)
        listed = jnp.where(lane % 8 < ENTRIES, listed, float(DEAD))
        refs = jnp.zeros((1, lanes), f32)
        for local in range(max(1, inner // SPAN)):
            scene = me_ref[0] * inner // SPAN + (local * SPAN + flip * me_ref[0]) % inner // SPAN
            ref_frame = scene * (SPAN * FRAMES_DEV) + ref_ref[scene]
            ref_dev = ref_frame // FRAMES_DEV
            ref_spot = (ref_dev % inner + flip * (ref_dev // inner)) % inner
            base = (ref_dev // inner) * units + ref_spot * n_tok * STRIDE
            for block in range(n_tok):
                which = base + block * STRIDE + ref_frame % FRAMES_DEV
                found = jnp.sum(jnp.where(lane == which, table, 0.0), axis=1, keepdims=True)
                refs = jnp.where(lane == local * n_tok + block, found, refs)
        return [listed, refs]

    rows = [sent, chosen + jnp.zeros_like(origin)] + places(spots) + places(everything)
    for index, row in enumerate(rows):
        out_ref[index : index + 1, :] = row.astype(jnp.int32)


def make_plan(epi_dev, epi_frame, epi_block, valid, ref_local, my_outer, inner, n_tok, flip, rooms):
    n_outer = epi_dev.shape[0] // (inner * FRAMES_DEV)
    n_units = n_outer * inner * n_tok * STRIDE
    lanes = -(-n_units // 128) * 128
    smem, anywhere = pl.BlockSpec(memory_space=pltpu.SMEM), pl.BlockSpec(memory_space=pl.ANY)
    return pl.pallas_call(
        functools.partial(plan_kernel, inner=inner, n_tok=n_tok, flip=flip, rooms=rooms),
        out_shape=jax.ShapeDtypeStruct((8, lanes), jnp.int32),
        in_specs=[smem, smem] + [anywhere] * 4,
        out_specs=WHOLE,
        scratch_shapes=[
            pltpu.VMEM((4,) + epi_dev.shape, jnp.int32),
            pltpu.SemaphoreType.DMA((4,)),
        ],
        compiler_params=pltpu.CompilerParams(vmem_limit_bytes=32 * 1024 * 1024),
    )(my_outer.reshape(1), ref_local, epi_dev, epi_frame, epi_block, valid)


def pack_kernel(plan_ref, own_ref, *targets):
    first = 0
    for target in targets:
        for slot in range(target.shape[0]):
            target[slot] = own_ref[plan_ref[0, first + slot]]
        first += target.shape[0]


def pack(plan, own, sizes):
    return pl.pallas_call(
        pack_kernel,
        out_shape=[jax.ShapeDtypeStruct((size,) + own.shape[1:], own.dtype) for size in sizes],
        grid_spec=pltpu.PrefetchScalarGridSpec(
            num_scalar_prefetch=1,
            grid=(),
            in_specs=[WHOLE],
            out_specs=[WHOLE] * len(sizes),
        ),
        compiler_params=pltpu.CompilerParams(vmem_limit_bytes=24 * 1024 * 1024),
        cost_estimate=pl.CostEstimate(
            flops=0, bytes_accessed=4 * sum(sizes) * own[0].size, transcendentals=0
        ),
    )(plan, own)


def part_of(pairs, query):
    scores = jnp.dot(pairs, query, preferred_element_type=jnp.float32)
    top = jnp.max(scores, axis=0, keepdims=True)
    weights = jnp.exp(scores - top)
    total = jnp.sum(weights, axis=0, keepdims=True)
    attended = jnp.dot(
        pairs.T[HEAD_DIM:], weights.astype(jnp.bfloat16), preferred_element_type=jnp.float32
    )
    return attended, top, total


def near_kernel(plan_ref, own_ref, query_ref, acc_ref, stat_ref, *, n_tok, spot_row, ref_near):
    n_local, n_tiles, _, tile = acc_ref.shape
    inner = n_local // FRAMES_DEV

    @pl.loop(0, inner, unroll=math.gcd(2, inner))
    def _(chip):
        spots = [(chip * n_tok + block) * STRIDE for block in range(n_tok)]
        refs = []
        if ref_near:
            scene = chip // SPAN * n_tok
            refs = [own_ref[plan_ref[spot_row + 1, scene + block]] for block in range(n_tok)]
        turned = [own_ref[spot + FRAMES_DEV].T for spot in spots]
        for frame in range(FRAMES_DEV):
            pairs = jnp.concatenate([own_ref[spot + frame] for spot in spots] + refs, 0)
            local = chip * FRAMES_DEV + frame
            for index in range(n_tiles):
                first = index * tile // BLOCK
                query = jnp.concatenate(
                    [
                        block[frame * HEAD_DIM : (frame + 1) * HEAD_DIM]
                        for block in turned[first : first + tile // BLOCK]
                    ],
                    1,
                ) * jnp.asarray(HEAD_DIM**-0.5, own_ref.dtype)
                query = jnp.concatenate([query, jnp.zeros_like(query)], 0)
                query_ref[local, index] = query
                attended, top, total = part_of(pairs, query)
                acc_ref[local, index] = attended
                stat_ref[local, index, 0:1] = top
                stat_ref[local, index, 1:2] = total


def near(plan, own, inner, n_tok, spot_row, ref_near):
    rows = n_tok * BLOCK
    tile = math.gcd(rows, 256)
    n_local = inner * FRAMES_DEV
    pairs = n_local * rows * (1 + ref_near) * rows
    lead = (n_local, rows // tile)
    return pl.pallas_call(
        functools.partial(near_kernel, n_tok=n_tok, spot_row=spot_row, ref_near=ref_near),
        out_shape=(
            jax.ShapeDtypeStruct(lead + (2 * HEAD_DIM, tile), own.dtype),
            jax.ShapeDtypeStruct(lead + (HEAD_DIM, tile), jnp.float32),
            jax.ShapeDtypeStruct(lead + (2, tile), jnp.float32),
        ),
        grid_spec=pltpu.PrefetchScalarGridSpec(
            num_scalar_prefetch=1,
            grid=(),
            in_specs=[WHOLE],
            out_specs=(WHOLE, WHOLE, WHOLE),
        ),
        compiler_params=pltpu.CompilerParams(vmem_limit_bytes=40 * 1024 * 1024),
        cost_estimate=pl.CostEstimate(
            flops=8 * pairs * HEAD_DIM,
            bytes_accessed=16 * n_local * rows * HEAD_DIM,
            transcendentals=pairs,
        ),
    )(plan, own)


def stage_kernel(
    plan_ref, query_ref, acc_in, stat_in, source_ref, *refs, low, high, spot_row, n_refs, final
):
    acc_ref, stat_ref, items = refs[-3:]
    n_local, n_tiles, _, tile = acc_ref.shape

    def add(found, local, code):
        items[found] = (local << 16) + (code - low)
        return found + ((code >= low) & (code < high)).astype(jnp.int32)

    def listed(local, found):
        for entry in range(ENTRIES):
            found = add(found, local, plan_ref[spot_row, local * 8 + entry])
        for block in range(n_refs):
            found = add(found, local, plan_ref[spot_row + 1, block])
        return found

    found = lax.fori_loop(0, n_local, listed, jnp.int32(0), unroll=math.gcd(2, n_local))

    @pl.loop(0, (found + (BATCH - 1)) >> BATCH_BITS)
    def _(step):
        for index in range(n_tiles):
            parts = []
            for turn in range(BATCH):
                here = step * BATCH + turn < found
                word = items[jnp.where(here, step * BATCH + turn, 0)]
                local = word >> 16
                parts.append((here, local, part_of(source_ref[word & (DEAD - 1)], query_ref[local, index])))
            for here, local, (attended, top, total) in parts:
                old_top = stat_ref[local, index, 0:1]
                new_top = jnp.where(here, jnp.maximum(old_top, top), old_top)
                keep = jnp.exp(old_top - new_top)
                add = jnp.where(here, jnp.exp(jnp.minimum(top - new_top, 0.0)), 0.0)
                acc_ref[local, index] = acc_ref[local, index] * keep + attended * add
                stat_ref[local, index, 1:2] = stat_ref[local, index, 1:2] * keep + total * add
                stat_ref[local, index, 0:1] = new_top

    if not final:
        return
    out_ref = refs[0]
    n_tok = n_tiles * tile // BLOCK
    inner = n_local // FRAMES_DEV

    @pl.loop(0, inner, unroll=math.gcd(4, inner))
    def _(chip):
        for index in range(n_tiles):
            parts = []
            for frame in range(FRAMES_DEV):
                local = chip * FRAMES_DEV + frame
                parts.append(acc_ref[local, index] * (1.0 / stat_ref[local, index][1:2]))
            result = jnp.concatenate(parts, 0).astype(out_ref.dtype).T
            for block in range(tile // BLOCK):
                out_ref[chip * n_tok + index * (tile // BLOCK) + block] = result[
                    block * BLOCK : (block + 1) * BLOCK
                ]


def stage(plan, source, query, acc, stat, low, n_ranks, spot_row, n_refs, final):
    out_shape = [jax.ShapeDtypeStruct(x.shape, x.dtype) for x in (acc, stat)]
    if final:
        result = jax.ShapeDtypeStruct((n_ranks, BLOCK, FRAMES_DEV * HEAD_DIM), query.dtype)
        out_shape = [result] + out_shape
    pairs = 2 * acc.size // HEAD_DIM * BLOCK
    return pl.pallas_call(
        functools.partial(
            stage_kernel, low=low, high=low + source.shape[0], spot_row=spot_row,
            n_refs=n_refs, final=final,
        ),
        out_shape=out_shape,
        grid_spec=pltpu.PrefetchScalarGridSpec(
            num_scalar_prefetch=1,
            grid=(),
            in_specs=[WHOLE] * 4,
            out_specs=[WHOLE] * len(out_shape),
            scratch_shapes=[pltpu.SMEM((acc.shape[0] * (8 + n_refs) + 1,), jnp.int32)],
        ),
        input_output_aliases={2: len(out_shape) - 2, 3: len(out_shape) - 1},
        compiler_params=pltpu.CompilerParams(vmem_limit_bytes=40 * 1024 * 1024),
        cost_estimate=pl.CostEstimate(
            flops=8 * pairs * HEAD_DIM, bytes_accessed=8 * acc.size, transcendentals=pairs
        ),
    )(plan, query, acc, stat, source)


def shards(queries, keys, values, epi_dev, epi_frame, epi_block, valid, ref_local, *, n_tm, n_tok):
    inner = HEADS // n_tok
    n_outer = n_tm // inner
    n_ranks = inner * n_tok
    units = n_ranks * STRIDE
    ref_near = inner % SPAN == 0
    n_refs = 0 if ref_near else n_tok
    blocks = n_ranks * FRAMES_DEV
    rooms = [-(-blocks * share // 16) for share in (10, 11, 12, 13, 14)] if n_outer == 2 else []
    flip = inner // 2 if n_outer == 2 and inner % (2 * SPAN) == 0 else 0

    def device(o, spot):
        return o * inner + (spot + flip * o) % inner

    groups = [
        [device(o, i) * n_tok + t for i in range(inner) for t in range(n_tok)]
        for o in range(n_outer)
    ]

    def exchange(x):
        return lax.all_to_all(x, ("tm", "tok"), 0, 0, axis_index_groups=groups, tiled=True)

    def turn(x):
        pairs = [
            (device(o, i), device((o + 1) % n_outer, i)) for o in range(n_outer) for i in range(inner)
        ]
        return lax.ppermute(x, "tm", pairs)

    my_outer = (lax.axis_index("tm") // inner).astype(jnp.int32)
    plan = make_plan(
        epi_dev, epi_frame, epi_block, valid, ref_local, my_outer, inner, n_tok, flip, rooms
    )
    small = pltpu.CompilerParams(vmem_limit_bytes=24 * 1024 * 1024)
    own = pl.pallas_call(
        split_kernel,
        out_shape=jax.ShapeDtypeStruct((n_ranks, STRIDE, BLOCK, 2 * HEAD_DIM), keys.dtype),
        in_specs=[pl.BlockSpec(memory_space=pltpu.HBM)] * 3,
        out_specs=WHOLE,
        scratch_shapes=[pltpu.VMEM(keys.shape, keys.dtype)] * 3 + [pltpu.SemaphoreType.DMA((3,))],
        compiler_params=small,
    )(*[pltpu.with_memory_space_constraint(x, pltpu.HBM) for x in (queries, keys, values)])
    own = exchange(own).reshape(units, BLOCK, 2 * HEAD_DIM)

    def attend(own, arrivals, spot_row, waiting=()):
        query, acc, stat = near(plan, own, inner, n_tok, spot_row, ref_near)
        acc, stat = stage(plan, own, query, acc, stat, 0, n_ranks, spot_row, n_refs, False)
        arrivals, waiting = list(arrivals), list(waiting)
        low = FAR
        while arrivals:
            if waiting:
                held, acc = lax.optimization_barrier((waiting.pop(0), acc))
                arrivals.append(turn(held))
            arrived = arrivals.pop(0)
            *result, acc, stat = stage(
                plan, arrived, query, acc, stat, low, n_ranks, spot_row, n_refs, not arrivals
            )
            low += arrived.shape[0]
        return result[0]

    def listed(room):
        sizes = (room - room // 2, room // 2 - room // 5, room // 5)

        def run(own):
            first, *later = pack(plan, own, sizes)
            return attend(own, [turn(first)], 2, later)

        return run

    def gathered(own):
        arrivals = [turn(own)]
        for _ in range(n_outer - 2):
            arrivals.append(turn(arrivals[-1]))
        return attend(own, arrivals, 4)

    options = [listed(room) for room in rooms] + [gathered]
    attended = exchange(lax.switch(plan[1, 0], options, own))
    return pl.pallas_call(
        merge_kernel,
        out_shape=jax.ShapeDtypeStruct(queries.shape, queries.dtype),
        in_specs=[WHOLE],
        out_specs=WHOLE,
        compiler_params=small,
    )(attended)


def solution(mesh):
    return jax.shard_map(
        functools.partial(shards, n_tm=mesh.shape["tm"], n_tok=mesh.shape["tok"]),
        mesh=mesh,
        in_specs=(P("tm", "tok", None),) * 3 + (P(),) * 5,
        out_specs=P("tm", "tok", None),
        check_vma=False,
    )
```

```python
import functools
import math

import jax
import jax.numpy as jnp
from jax import lax
from jax.experimental import pallas as pl
from jax.experimental.pallas import tpu as pltpu
from jax.sharding import PartitionSpec as P

HEADS = 16
HEAD_DIM = 64
BLOCK = 128
FRAMES_DEV = 2
ENTRIES = 6
SPAN = 4
FAR = 1024
DEAD = 65536
BATCH_BITS = 2
BATCH = 1 << BATCH_BITS

STRIDE = FRAMES_DEV + 1
WHOLE = pl.BlockSpec(memory_space=pltpu.VMEM)


def split_kernel(q_hbm, k_hbm, v_hbm, out_ref, q_ref, k_ref, v_ref, sems):
    copies = [
        pltpu.make_async_copy(source, target, sems.at[index])
        for index, (source, target) in enumerate(
            ((q_hbm, q_ref), (k_hbm, k_ref), (v_hbm, v_ref))
        )
    ]
    for copy in copies:
        copy.start()
    copies[0].wait()
    lanes_of = [slice(rank * HEAD_DIM, (rank + 1) * HEAD_DIM) for rank in range(out_ref.shape[0])]
    for rank, lanes in enumerate(lanes_of):
        out_ref[rank, FRAMES_DEV] = jnp.concatenate(
            [q_ref[frame, :, lanes] for frame in range(FRAMES_DEV)], 1
        )
    for copy in copies[1:]:
        copy.wait()
    for rank, lanes in enumerate(lanes_of):
        for frame in range(FRAMES_DEV):
            out_ref[rank, frame] = jnp.concatenate(
                [k_ref[frame, :, lanes], v_ref[frame, :, lanes]], 1
            )


def merge_kernel(x_ref, out_ref):
    for frame in range(FRAMES_DEV):
        part = slice(frame * HEAD_DIM, (frame + 1) * HEAD_DIM)
        for rank in range(0, x_ref.shape[0], 2):
            out_ref[frame, :, rank * HEAD_DIM : (rank + 2) * HEAD_DIM] = jnp.concatenate(
                [x_ref[rank, :, part], x_ref[rank + 1, :, part]], 1
            )


def plan_kernel(
    me_ref, ref_ref, dev_hbm, place_hbm, block_hbm, valid_hbm, out_ref, entries, sems,
    *, inner, n_tok, flip, rooms,
):
    copies = [
        pltpu.make_async_copy(array, entries.at[index], sems.at[index])
        for index, array in enumerate((dev_hbm, place_hbm, block_hbm, valid_hbm))
    ]
    for copy in copies:
        copy.start()
    for copy in copies:
        copy.wait()
    n_frames = dev_hbm.shape[0]
    units = inner * n_tok * STRIDE
    group_frames = inner * FRAMES_DEV
    n_outer = n_frames // group_frames
    lanes = out_ref.shape[1]
    f32 = jnp.float32
    me = me_ref[0].astype(f32)
    dev = entries[0]
    spot = (dev % inner + flip * (dev // inner)) % inner
    ids = (dev // inner) * units + (spot * n_tok + entries[2]) * STRIDE + entries[1]
    used = entries[3] > 0
    frame_lane = lax.broadcasted_iota(jnp.int32, (n_frames, lanes), 1)
    hit = jnp.zeros((n_frames, lanes), f32)
    for entry in range(ENTRIES):
        here = (ids[:, entry : entry + 1] == frame_lane) & used[:, entry : entry + 1]
        hit = jnp.where(here, 1.0, hit)
    lane = lax.broadcasted_iota(jnp.int32, (1, lanes), 1)
    unit = (lane % units).astype(f32)
    origin = (lane // units).astype(f32)
    crosses = jnp.zeros((1, lanes), f32)
    for group in range(n_outer):
        rows = lax.slice_in_dim(hit, group * group_frames, (group + 1) * group_frames)
        wanted = jnp.max(rows, axis=0, keepdims=True)
        crosses = jnp.where(origin != group, jnp.maximum(wanted, crosses), crosses)

    def count(mask, axis):
        return jnp.sum(jnp.where(mask, 1.0, 0.0), axis=axis, keepdims=True)

    steps = jnp.where(origin > me, me - origin + n_outer, me - origin)
    everything = jnp.where(origin == me, unit, FAR + (steps - 1.0) * units + unit)
    sent, spots, chosen = jnp.zeros_like(origin), everything, jnp.full((1, 1), float(len(rooms)), f32)
    if rooms:
        square_row = lax.broadcasted_iota(jnp.int32, (lanes, lanes), 0)
        square_lane = lax.broadcasted_iota(jnp.int32, (lanes, lanes), 1)

        def column(row):
            return jnp.sum(jnp.where(square_row == square_lane, row, 0.0), axis=1, keepdims=True)

        key = jnp.where(crosses > 0, origin, -1.0)
        slot = count((column(key) == key) & (square_row < square_lane), 0)
        most = jnp.max(jnp.where(crosses > 0, slot + 1.0, 0.0), axis=1, keepdims=True)
        for index in reversed(range(len(rooms))):
            chosen = jnp.where(most <= rooms[index], float(index), chosen)
        mine = column(jnp.where((crosses > 0) & (origin == me), slot, -1.0))
        sent = jnp.sum(
            jnp.where(mine == square_lane.astype(f32), column(unit), 0.0), axis=0, keepdims=True
        )
        spots = jnp.where(origin == me, unit, FAR + slot)

    row_frame = lax.broadcasted_iota(jnp.int32, (n_frames, lanes), 0).astype(f32)
    wide_lane = frame_lane.astype(f32)
    local_row = row_frame - me * group_frames
    turned = local_row + me * (flip * FRAMES_DEV)
    turned = jnp.where(turned >= group_frames, turned - group_frames, turned) * 8
    turned = jnp.where((local_row >= 0) & (local_row < group_frames), turned, -8.0)

    def places(table):
        listed = jnp.zeros((1, lanes), f32)
        for entry in range(ENTRIES):
            mine, live = ids[:, entry : entry + 1], used[:, entry : entry + 1]
            found = jnp.sum(jnp.where(mine == frame_lane, table, 0.0), axis=1, keepdims=True)
            found = jnp.where(live, found, float(DEAD))
            target = turned + entry
            listed += jnp.sum(jnp.where(target == wide_lane, found, 0.0), axis=0, keepdims=True)
        listed = jnp.where(lane % 8 < ENTRIES, listed, float(DEAD))
        refs = jnp.zeros((1, lanes), f32)
        for local in range(max(1, inner // SPAN)):
            scene = me_ref[0] * inner // SPAN + (local * SPAN + flip * me_ref[0]) % inner // SPAN
            ref_frame = scene * (SPAN * FRAMES_DEV) + ref_ref[scene]
            ref_dev = ref_frame // FRAMES_DEV
            ref_spot = (ref_dev % inner + flip * (ref_dev // inner)) % inner
            base = (ref_dev // inner) * units + ref_spot * n_tok * STRIDE
            for block in range(n_tok):
                which = base + block * STRIDE + ref_frame % FRAMES_DEV
                found = jnp.sum(jnp.where(lane == which, table, 0.0), axis=1, keepdims=True)
                refs = jnp.where(lane == local * n_tok + block, found, refs)
        return [listed, refs]

    rows = [sent, chosen + jnp.zeros_like(origin)] + places(spots) + places(everything)
    for index, row in enumerate(rows):
        out_ref[index : index + 1, :] = row.astype(jnp.int32)


def make_plan(epi_dev, epi_frame, epi_block, valid, ref_local, my_outer, inner, n_tok, flip, rooms):
    n_outer = epi_dev.shape[0] // (inner * FRAMES_DEV)
    n_units = n_outer * inner * n_tok * STRIDE
    lanes = -(-n_units // 128) * 128
    smem, anywhere = pl.BlockSpec(memory_space=pltpu.SMEM), pl.BlockSpec(memory_space=pl.ANY)
    return pl.pallas_call(
        functools.partial(plan_kernel, inner=inner, n_tok=n_tok, flip=flip, rooms=rooms),
        out_shape=jax.ShapeDtypeStruct((8, lanes), jnp.int32),
        in_specs=[smem, smem] + [anywhere] * 4,
        out_specs=WHOLE,
        scratch_shapes=[
            pltpu.VMEM((4,) + epi_dev.shape, jnp.int32),
            pltpu.SemaphoreType.DMA((4,)),
        ],
        compiler_params=pltpu.CompilerParams(vmem_limit_bytes=32 * 1024 * 1024),
    )(my_outer.reshape(1), ref_local, epi_dev, epi_frame, epi_block, valid)


def pack_kernel(plan_ref, own_ref, *targets):
    first = 0
    for target in targets:
        for slot in range(target.shape[0]):
            target[slot] = own_ref[plan_ref[0, first + slot]]
        first += target.shape[0]


def pack(plan, own, sizes):
    return pl.pallas_call(
        pack_kernel,
        out_shape=[jax.ShapeDtypeStruct((size,) + own.shape[1:], own.dtype) for size in sizes],
        grid_spec=pltpu.PrefetchScalarGridSpec(
            num_scalar_prefetch=1,
            grid=(),
            in_specs=[WHOLE],
            out_specs=[WHOLE] * len(sizes),
        ),
        compiler_params=pltpu.CompilerParams(vmem_limit_bytes=24 * 1024 * 1024),
        cost_estimate=pl.CostEstimate(
            flops=0, bytes_accessed=4 * sum(sizes) * own[0].size, transcendentals=0
        ),
    )(plan, own)


def part_of(pairs, query):
    scores = jnp.dot(pairs, query, preferred_element_type=jnp.float32)
    top = jnp.max(scores, axis=0, keepdims=True)
    weights = jnp.exp(scores - top)
    total = jnp.sum(weights, axis=0, keepdims=True)
    attended = jnp.dot(
        pairs.T[HEAD_DIM:], weights.astype(jnp.bfloat16), preferred_element_type=jnp.float32
    )
    return attended, top, total


def near_kernel(plan_ref, own_ref, query_ref, acc_ref, stat_ref, *, n_tok, spot_row, ref_near):
    n_local, n_tiles, _, tile = acc_ref.shape
    inner = n_local // FRAMES_DEV

    @pl.loop(0, inner, unroll=math.gcd(2, inner))
    def _(chip):
        spots = [(chip * n_tok + block) * STRIDE for block in range(n_tok)]
        refs = []
        if ref_near:
            scene = chip // SPAN * n_tok
            refs = [own_ref[plan_ref[spot_row + 1, scene + block]] for block in range(n_tok)]
        turned = [own_ref[spot + FRAMES_DEV].T for spot in spots]
        for frame in range(FRAMES_DEV):
            pairs = jnp.concatenate([own_ref[spot + frame] for spot in spots] + refs, 0)
            local = chip * FRAMES_DEV + frame
            for index in range(n_tiles):
                first = index * tile // BLOCK
                query = jnp.concatenate(
                    [
                        block[frame * HEAD_DIM : (frame + 1) * HEAD_DIM]
                        for block in turned[first : first + tile // BLOCK]
                    ],
                    1,
                ) * jnp.asarray(HEAD_DIM**-0.5, own_ref.dtype)
                query = jnp.concatenate([query, jnp.zeros_like(query)], 0)
                query_ref[local, index] = query
                attended, top, total = part_of(pairs, query)
                acc_ref[local, index] = attended
                stat_ref[local, index, 0:1] = top
                stat_ref[local, index, 1:2] = total


def near(plan, own, inner, n_tok, spot_row, ref_near):
    rows = n_tok * BLOCK
    tile = math.gcd(rows, 256)
    n_local = inner * FRAMES_DEV
    pairs = n_local * rows * (1 + ref_near) * rows
    lead = (n_local, rows // tile)
    return pl.pallas_call(
        functools.partial(near_kernel, n_tok=n_tok, spot_row=spot_row, ref_near=ref_near),
        out_shape=(
            jax.ShapeDtypeStruct(lead + (2 * HEAD_DIM, tile), own.dtype),
            jax.ShapeDtypeStruct(lead + (HEAD_DIM, tile), jnp.float32),
            jax.ShapeDtypeStruct(lead + (2, tile), jnp.float32),
        ),
        grid_spec=pltpu.PrefetchScalarGridSpec(
            num_scalar_prefetch=1,
            grid=(),
            in_specs=[WHOLE],
            out_specs=(WHOLE, WHOLE, WHOLE),
        ),
        compiler_params=pltpu.CompilerParams(vmem_limit_bytes=40 * 1024 * 1024),
        cost_estimate=pl.CostEstimate(
            flops=8 * pairs * HEAD_DIM,
            bytes_accessed=16 * n_local * rows * HEAD_DIM,
            transcendentals=pairs,
        ),
    )(plan, own)


def stage_kernel(
    plan_ref, query_ref, acc_in, stat_in, source_ref, *refs, low, high, spot_row, n_refs, final
):
    acc_ref, stat_ref, items = refs[-3:]
    n_local, n_tiles, _, tile = acc_ref.shape

    def add(found, local, code):
        items[found] = (local << 16) + (code - low)
        return found + ((code >= low) & (code < high)).astype(jnp.int32)

    def listed(local, found):
        for entry in range(ENTRIES):
            found = add(found, local, plan_ref[spot_row, local * 8 + entry])
        for block in range(n_refs):
            found = add(found, local, plan_ref[spot_row + 1, block])
        return found

    found = lax.fori_loop(0, n_local, listed, jnp.int32(0), unroll=math.gcd(2, n_local))

    @pl.loop(0, (found + (BATCH - 1)) >> BATCH_BITS)
    def _(step):
        for index in range(n_tiles):
            parts = []
            for turn in range(BATCH):
                here = step * BATCH + turn < found
                word = items[jnp.where(here, step * BATCH + turn, 0)]
                local = word >> 16
                parts.append((here, local, part_of(source_ref[word & (DEAD - 1)], query_ref[local, index])))
            for here, local, (attended, top, total) in parts:
                old_top = stat_ref[local, index, 0:1]
                new_top = jnp.where(here, jnp.maximum(old_top, top), old_top)
                keep = jnp.exp(old_top - new_top)
                add = jnp.where(here, jnp.exp(jnp.minimum(top - new_top, 0.0)), 0.0)
                acc_ref[local, index] = acc_ref[local, index] * keep + attended * add
                stat_ref[local, index, 1:2] = stat_ref[local, index, 1:2] * keep + total * add
                stat_ref[local, index, 0:1] = new_top

    if not final:
        return
    out_ref = refs[0]
    n_tok = n_tiles * tile // BLOCK
    inner = n_local // FRAMES_DEV

    @pl.loop(0, inner, unroll=math.gcd(4, inner))
    def _(chip):
        for index in range(n_tiles):
            parts = []
            for frame in range(FRAMES_DEV):
                local = chip * FRAMES_DEV + frame
                parts.append(acc_ref[local, index] * (1.0 / stat_ref[local, index][1:2]))
            result = jnp.concatenate(parts, 0).astype(out_ref.dtype).T
            for block in range(tile // BLOCK):
                out_ref[chip * n_tok + index * (tile // BLOCK) + block] = result[
                    block * BLOCK : (block + 1) * BLOCK
                ]


def stage(plan, source, query, acc, stat, low, n_ranks, spot_row, n_refs, final):
    out_shape = [jax.ShapeDtypeStruct(x.shape, x.dtype) for x in (acc, stat)]
    if final:
        result = jax.ShapeDtypeStruct((n_ranks, BLOCK, FRAMES_DEV * HEAD_DIM), query.dtype)
        out_shape = [result] + out_shape
    pairs = 2 * acc.size // HEAD_DIM * BLOCK
    return pl.pallas_call(
        functools.partial(
            stage_kernel, low=low, high=low + source.shape[0], spot_row=spot_row,
            n_refs=n_refs, final=final,
        ),
        out_shape=out_shape,
        grid_spec=pltpu.PrefetchScalarGridSpec(
            num_scalar_prefetch=1,
            grid=(),
            in_specs=[WHOLE] * 4,
            out_specs=[WHOLE] * len(out_shape),
            scratch_shapes=[pltpu.SMEM((acc.shape[0] * (8 + n_refs) + 1,), jnp.int32)],
        ),
        input_output_aliases={2: len(out_shape) - 2, 3: len(out_shape) - 1},
        compiler_params=pltpu.CompilerParams(vmem_limit_bytes=40 * 1024 * 1024),
        cost_estimate=pl.CostEstimate(
            flops=8 * pairs * HEAD_DIM, bytes_accessed=8 * acc.size, transcendentals=pairs
        ),
    )(plan, query, acc, stat, source)


def shards(queries, keys, values, epi_dev, epi_frame, epi_block, valid, ref_local, *, n_tm, n_tok):
    inner = HEADS // n_tok
    n_outer = n_tm // inner
    n_ranks = inner * n_tok
    units = n_ranks * STRIDE
    ref_near = inner % SPAN == 0
    n_refs = 0 if ref_near else n_tok
    blocks = n_ranks * FRAMES_DEV
    rooms = [-(-blocks * share // 32) for share in (*range(19, 27), 28)] if n_outer == 2 else []
    flip = inner // 2 if n_outer == 2 and inner % (2 * SPAN) == 0 else 0

    def device(o, spot):
        return o * inner + (spot + flip * o) % inner

    groups = [
        [device(o, i) * n_tok + t for i in range(inner) for t in range(n_tok)]
        for o in range(n_outer)
    ]

    def exchange(x):
        return lax.all_to_all(x, ("tm", "tok"), 0, 0, axis_index_groups=groups, tiled=True)

    def turn(x):
        pairs = [
            (device(o, i), device((o + 1) % n_outer, i)) for o in range(n_outer) for i in range(inner)
        ]
        return lax.ppermute(x, "tm", pairs)

    my_outer = (lax.axis_index("tm") // inner).astype(jnp.int32)
    plan = make_plan(
        epi_dev, epi_frame, epi_block, valid, ref_local, my_outer, inner, n_tok, flip, rooms
    )
    small = pltpu.CompilerParams(vmem_limit_bytes=24 * 1024 * 1024)
    own = pl.pallas_call(
        split_kernel,
        out_shape=jax.ShapeDtypeStruct((n_ranks, STRIDE, BLOCK, 2 * HEAD_DIM), keys.dtype),
        in_specs=[pl.BlockSpec(memory_space=pltpu.HBM)] * 3,
        out_specs=WHOLE,
        scratch_shapes=[pltpu.VMEM(keys.shape, keys.dtype)] * 3 + [pltpu.SemaphoreType.DMA((3,))],
        compiler_params=small,
    )(*[pltpu.with_memory_space_constraint(x, pltpu.HBM) for x in (queries, keys, values)])
    own = exchange(own).reshape(units, BLOCK, 2 * HEAD_DIM)

    def attend(own, arrivals, spot_row, waiting=()):
        query, acc, stat = near(plan, own, inner, n_tok, spot_row, ref_near)
        acc, stat = stage(plan, own, query, acc, stat, 0, n_ranks, spot_row, n_refs, False)
        arrivals, waiting = list(arrivals), list(waiting)
        low = FAR
        while arrivals:
            if waiting:
                held, acc = lax.optimization_barrier((waiting.pop(0), acc))
                arrivals.append(turn(held))
            arrived = arrivals.pop(0)
            *result, acc, stat = stage(
                plan, arrived, query, acc, stat, low, n_ranks, spot_row, n_refs, not arrivals
            )
            low += arrived.shape[0]
        return result[0]

    def listed(room):
        sizes = (room - room * 2 // 5, room * 2 // 5)

        def run(own):
            first, *later = pack(plan, own, sizes)
            return attend(own, [turn(first)], 2, later)

        return run

    def gathered(own):
        arrivals = [turn(own)]
        for _ in range(n_outer - 2):
            arrivals.append(turn(arrivals[-1]))
        return attend(own, arrivals, 4)

    options = [listed(room) for room in rooms] + [gathered]
    attended = exchange(lax.switch(plan[1, 0], options, own))
    return pl.pallas_call(
        merge_kernel,
        out_shape=jax.ShapeDtypeStruct(queries.shape, queries.dtype),
        in_specs=[WHOLE],
        out_specs=WHOLE,
        compiler_params=small,
    )(attended)


def solution(mesh):
    return jax.shard_map(
        functools.partial(shards, n_tm=mesh.shape["tm"], n_tok=mesh.shape["tok"]),
        mesh=mesh,
        in_specs=(P("tm", "tok", None),) * 3 + (P(),) * 5,
        out_specs=P("tm", "tok", None),
        check_vma=False,
    )
```

```python
import functools
import math

import jax
import jax.numpy as jnp
from jax import lax
from jax.experimental import pallas as pl
from jax.experimental.pallas import tpu as pltpu
from jax.sharding import PartitionSpec as P

HEADS = 16
HEAD_DIM = 64
BLOCK = 128
FRAMES_DEV = 2
ENTRIES = 6
SPAN = 4
FAR = 1024
DEAD = 65536
BATCH_BITS = 2
BATCH = 1 << BATCH_BITS

STRIDE = FRAMES_DEV + 1
WHOLE = pl.BlockSpec(memory_space=pltpu.VMEM)


def split_kernel(q_hbm, k_hbm, v_hbm, out_ref, q_ref, k_ref, v_ref, sems):
    copies = [
        pltpu.make_async_copy(source, target, sems.at[index])
        for index, (source, target) in enumerate(
            ((q_hbm, q_ref), (k_hbm, k_ref), (v_hbm, v_ref))
        )
    ]
    for copy in copies:
        copy.start()
    copies[0].wait()
    lanes_of = [slice(rank * HEAD_DIM, (rank + 1) * HEAD_DIM) for rank in range(out_ref.shape[0])]
    for rank, lanes in enumerate(lanes_of):
        out_ref[rank, FRAMES_DEV] = jnp.concatenate(
            [q_ref[frame, :, lanes] for frame in range(FRAMES_DEV)], 1
        )
    for copy in copies[1:]:
        copy.wait()
    for rank, lanes in enumerate(lanes_of):
        for frame in range(FRAMES_DEV):
            out_ref[rank, frame] = jnp.concatenate(
                [k_ref[frame, :, lanes], v_ref[frame, :, lanes]], 1
            )


def merge_kernel(x_ref, out_ref):
    for frame in range(FRAMES_DEV):
        part = slice(frame * HEAD_DIM, (frame + 1) * HEAD_DIM)
        for rank in range(0, x_ref.shape[0], 2):
            out_ref[frame, :, rank * HEAD_DIM : (rank + 2) * HEAD_DIM] = jnp.concatenate(
                [x_ref[rank, :, part], x_ref[rank + 1, :, part]], 1
            )


def plan_kernel(
    me_ref, ref_ref, dev_hbm, place_hbm, block_hbm, valid_hbm, out_ref, entries, sems,
    *, inner, n_tok, flip, rooms,
):
    copies = [
        pltpu.make_async_copy(array, entries.at[index], sems.at[index])
        for index, array in enumerate((dev_hbm, place_hbm, block_hbm, valid_hbm))
    ]
    for copy in copies:
        copy.start()
    for copy in copies:
        copy.wait()
    n_frames = dev_hbm.shape[0]
    units = inner * n_tok * STRIDE
    group_frames = inner * FRAMES_DEV
    n_outer = n_frames // group_frames
    lanes = out_ref.shape[1]
    f32 = jnp.float32
    me = me_ref[0].astype(f32)
    dev = entries[0]
    spot = (dev % inner + flip * (dev // inner)) % inner
    ids = (dev // inner) * units + (spot * n_tok + entries[2]) * STRIDE + entries[1]
    used = entries[3] > 0
    frame_lane = lax.broadcasted_iota(jnp.int32, (n_frames, lanes), 1)
    hit = jnp.zeros((n_frames, lanes), f32)
    for entry in range(ENTRIES):
        here = (ids[:, entry : entry + 1] == frame_lane) & used[:, entry : entry + 1]
        hit = jnp.where(here, 1.0, hit)
    lane = lax.broadcasted_iota(jnp.int32, (1, lanes), 1)
    unit = (lane % units).astype(f32)
    origin = (lane // units).astype(f32)
    crosses = jnp.zeros((1, lanes), f32)
    for group in range(n_outer):
        rows = lax.slice_in_dim(hit, group * group_frames, (group + 1) * group_frames)
        wanted = jnp.sum(rows, axis=0, keepdims=True)
        crosses = jnp.where(origin != group, wanted + crosses, crosses)

    def count(mask, axis):
        return jnp.sum(jnp.where(mask, 1.0, 0.0), axis=axis, keepdims=True)

    steps = jnp.where(origin > me, me - origin + n_outer, me - origin)
    everything = jnp.where(origin == me, unit, FAR + (steps - 1.0) * units + unit)
    sent, spots, chosen = jnp.zeros_like(origin), everything, jnp.full((1, 1), float(len(rooms)), f32)
    if rooms:
        square_row = lax.broadcasted_iota(jnp.int32, (lanes, lanes), 0)
        square_lane = lax.broadcasted_iota(jnp.int32, (lanes, lanes), 1)

        def column(row):
            return jnp.sum(jnp.where(square_row == square_lane, row, 0.0), axis=1, keepdims=True)

        key = jnp.where(crosses > 0, origin, -1.0)
        uses = column(crosses)
        ahead = (uses > crosses) | ((uses == crosses) & (square_row < square_lane))
        slot = count((column(key) == key) & ahead, 0)
        most = jnp.max(jnp.where(crosses > 0, slot + 1.0, 0.0), axis=1, keepdims=True)
        for index in reversed(range(len(rooms))):
            chosen = jnp.where(most <= rooms[index], float(index), chosen)
        mine = column(jnp.where((crosses > 0) & (origin == me), slot, -1.0))
        sent = jnp.sum(
            jnp.where(mine == square_lane.astype(f32), column(unit), 0.0), axis=0, keepdims=True
        )
        spots = jnp.where(origin == me, unit, FAR + slot)

    row_frame = lax.broadcasted_iota(jnp.int32, (n_frames, lanes), 0).astype(f32)
    wide_lane = frame_lane.astype(f32)
    local_row = row_frame - me * group_frames
    turned = local_row + me * (flip * FRAMES_DEV)
    turned = jnp.where(turned >= group_frames, turned - group_frames, turned) * 8
    turned = jnp.where((local_row >= 0) & (local_row < group_frames), turned, -8.0)

    def places(table):
        listed = jnp.zeros((1, lanes), f32)
        for entry in range(ENTRIES):
            mine, live = ids[:, entry : entry + 1], used[:, entry : entry + 1]
            found = jnp.sum(jnp.where(mine == frame_lane, table, 0.0), axis=1, keepdims=True)
            found = jnp.where(live, found, float(DEAD))
            target = turned + entry
            listed += jnp.sum(jnp.where(target == wide_lane, found, 0.0), axis=0, keepdims=True)
        listed = jnp.where(lane % 8 < ENTRIES, listed, float(DEAD))
        refs = jnp.zeros((1, lanes), f32)
        for local in range(max(1, inner // SPAN)):
            scene = me_ref[0] * inner // SPAN + (local * SPAN + flip * me_ref[0]) % inner // SPAN
            ref_frame = scene * (SPAN * FRAMES_DEV) + ref_ref[scene]
            ref_dev = ref_frame // FRAMES_DEV
            ref_spot = (ref_dev % inner + flip * (ref_dev // inner)) % inner
            base = (ref_dev // inner) * units + ref_spot * n_tok * STRIDE
            for block in range(n_tok):
                which = base + block * STRIDE + ref_frame % FRAMES_DEV
                found = jnp.sum(jnp.where(lane == which, table, 0.0), axis=1, keepdims=True)
                refs = jnp.where(lane == local * n_tok + block, found, refs)
        return [listed, refs]

    rows = [sent, chosen + jnp.zeros_like(origin)] + places(spots) + places(everything)
    for index, row in enumerate(rows):
        out_ref[index : index + 1, :] = row.astype(jnp.int32)


def make_plan(epi_dev, epi_frame, epi_block, valid, ref_local, my_outer, inner, n_tok, flip, rooms):
    n_outer = epi_dev.shape[0] // (inner * FRAMES_DEV)
    n_units = n_outer * inner * n_tok * STRIDE
    lanes = -(-n_units // 128) * 128
    smem, anywhere = pl.BlockSpec(memory_space=pltpu.SMEM), pl.BlockSpec(memory_space=pl.ANY)
    return pl.pallas_call(
        functools.partial(plan_kernel, inner=inner, n_tok=n_tok, flip=flip, rooms=rooms),
        out_shape=jax.ShapeDtypeStruct((8, lanes), jnp.int32),
        in_specs=[smem, smem] + [anywhere] * 4,
        out_specs=WHOLE,
        scratch_shapes=[
            pltpu.VMEM((4,) + epi_dev.shape, jnp.int32),
            pltpu.SemaphoreType.DMA((4,)),
        ],
        compiler_params=pltpu.CompilerParams(vmem_limit_bytes=32 * 1024 * 1024),
    )(my_outer.reshape(1), ref_local, epi_dev, epi_frame, epi_block, valid)


def pack_kernel(plan_ref, own_ref, *targets):
    first = 0
    for target in targets:
        for slot in range(target.shape[0]):
            target[slot] = own_ref[plan_ref[0, first + slot]]
        first += target.shape[0]


def pack(plan, own, sizes):
    return pl.pallas_call(
        pack_kernel,
        out_shape=[jax.ShapeDtypeStruct((size,) + own.shape[1:], own.dtype) for size in sizes],
        grid_spec=pltpu.PrefetchScalarGridSpec(
            num_scalar_prefetch=1,
            grid=(),
            in_specs=[WHOLE],
            out_specs=[WHOLE] * len(sizes),
        ),
        compiler_params=pltpu.CompilerParams(vmem_limit_bytes=24 * 1024 * 1024),
        cost_estimate=pl.CostEstimate(
            flops=0, bytes_accessed=4 * sum(sizes) * own[0].size, transcendentals=0
        ),
    )(plan, own)


def part_of(pairs, query):
    scores = jnp.dot(pairs, query, preferred_element_type=jnp.float32)
    top = jnp.max(scores, axis=0, keepdims=True)
    weights = jnp.exp(scores - top)
    total = jnp.sum(weights, axis=0, keepdims=True)
    attended = jnp.dot(
        pairs.T[HEAD_DIM:], weights.astype(jnp.bfloat16), preferred_element_type=jnp.float32
    )
    return attended, top, total


def near_kernel(plan_ref, own_ref, query_ref, acc_ref, stat_ref, *, n_tok, spot_row, ref_near):
    n_local, n_tiles, _, tile = acc_ref.shape
    inner = n_local // FRAMES_DEV

    @pl.loop(0, inner, unroll=math.gcd(2, inner))
    def _(chip):
        spots = [(chip * n_tok + block) * STRIDE for block in range(n_tok)]
        refs = []
        if ref_near:
            scene = chip // SPAN * n_tok
            refs = [own_ref[plan_ref[spot_row + 1, scene + block]] for block in range(n_tok)]
        turned = [own_ref[spot + FRAMES_DEV].T for spot in spots]
        for frame in range(FRAMES_DEV):
            pairs = jnp.concatenate([own_ref[spot + frame] for spot in spots] + refs, 0)
            local = chip * FRAMES_DEV + frame
            for index in range(n_tiles):
                first = index * tile // BLOCK
                query = jnp.concatenate(
                    [
                        block[frame * HEAD_DIM : (frame + 1) * HEAD_DIM]
                        for block in turned[first : first + tile // BLOCK]
                    ],
                    1,
                ) * jnp.asarray(HEAD_DIM**-0.5, own_ref.dtype)
                query = jnp.concatenate([query, jnp.zeros_like(query)], 0)
                query_ref[local, index] = query
                attended, top, total = part_of(pairs, query)
                acc_ref[local, index] = attended
                stat_ref[local, index, 0:1] = top
                stat_ref[local, index, 1:2] = total


def near(plan, own, inner, n_tok, spot_row, ref_near):
    rows = n_tok * BLOCK
    tile = math.gcd(rows, 256)
    n_local = inner * FRAMES_DEV
    pairs = n_local * rows * (1 + ref_near) * rows
    lead = (n_local, rows // tile)
    return pl.pallas_call(
        functools.partial(near_kernel, n_tok=n_tok, spot_row=spot_row, ref_near=ref_near),
        out_shape=(
            jax.ShapeDtypeStruct(lead + (2 * HEAD_DIM, tile), own.dtype),
            jax.ShapeDtypeStruct(lead + (HEAD_DIM, tile), jnp.float32),
            jax.ShapeDtypeStruct(lead + (2, tile), jnp.float32),
        ),
        grid_spec=pltpu.PrefetchScalarGridSpec(
            num_scalar_prefetch=1,
            grid=(),
            in_specs=[WHOLE],
            out_specs=(WHOLE, WHOLE, WHOLE),
        ),
        compiler_params=pltpu.CompilerParams(vmem_limit_bytes=40 * 1024 * 1024),
        cost_estimate=pl.CostEstimate(
            flops=8 * pairs * HEAD_DIM,
            bytes_accessed=16 * n_local * rows * HEAD_DIM,
            transcendentals=pairs,
        ),
    )(plan, own)


def stage_kernel(
    plan_ref, query_ref, acc_in, stat_in, source_ref, *refs, low, high, spot_row, n_refs, final
):
    acc_ref, stat_ref, items = refs[-3:]
    n_local, n_tiles, _, tile = acc_ref.shape

    def add(found, local, code):
        items[found] = (local << 16) + (code - low)
        return found + ((code >= low) & (code < high)).astype(jnp.int32)

    def listed(local, found):
        for entry in range(ENTRIES):
            found = add(found, local, plan_ref[spot_row, local * 8 + entry])
        for block in range(n_refs):
            found = add(found, local, plan_ref[spot_row + 1, block])
        return found

    found = lax.fori_loop(0, n_local, listed, jnp.int32(0), unroll=math.gcd(2, n_local))

    @pl.loop(0, (found + (BATCH - 1)) >> BATCH_BITS)
    def _(step):
        for index in range(n_tiles):
            parts = []
            for turn in range(BATCH):
                here = step * BATCH + turn < found
                word = items[jnp.where(here, step * BATCH + turn, 0)]
                local = word >> 16
                parts.append((here, local, part_of(source_ref[word & (DEAD - 1)], query_ref[local, index])))
            for here, local, (attended, top, total) in parts:
                old_top = stat_ref[local, index, 0:1]
                new_top = jnp.where(here, jnp.maximum(old_top, top), old_top)
                keep = jnp.exp(old_top - new_top)
                add = jnp.where(here, jnp.exp(jnp.minimum(top - new_top, 0.0)), 0.0)
                acc_ref[local, index] = acc_ref[local, index] * keep + attended * add
                stat_ref[local, index, 1:2] = stat_ref[local, index, 1:2] * keep + total * add
                stat_ref[local, index, 0:1] = new_top

    if not final:
        return
    out_ref = refs[0]
    n_tok = n_tiles * tile // BLOCK
    inner = n_local // FRAMES_DEV

    @pl.loop(0, inner, unroll=math.gcd(4, inner))
    def _(chip):
        for index in range(n_tiles):
            parts = []
            for frame in range(FRAMES_DEV):
                local = chip * FRAMES_DEV + frame
                parts.append(acc_ref[local, index] * (1.0 / stat_ref[local, index][1:2]))
            result = jnp.concatenate(parts, 0).astype(out_ref.dtype).T
            for block in range(tile // BLOCK):
                out_ref[chip * n_tok + index * (tile // BLOCK) + block] = result[
                    block * BLOCK : (block + 1) * BLOCK
                ]


def stage(plan, source, query, acc, stat, low, n_ranks, spot_row, n_refs, final):
    out_shape = [jax.ShapeDtypeStruct(x.shape, x.dtype) for x in (acc, stat)]
    if final:
        result = jax.ShapeDtypeStruct((n_ranks, BLOCK, FRAMES_DEV * HEAD_DIM), query.dtype)
        out_shape = [result] + out_shape
    pairs = 2 * acc.size // HEAD_DIM * BLOCK
    return pl.pallas_call(
        functools.partial(
            stage_kernel, low=low, high=low + source.shape[0], spot_row=spot_row,
            n_refs=n_refs, final=final,
        ),
        out_shape=out_shape,
        grid_spec=pltpu.PrefetchScalarGridSpec(
            num_scalar_prefetch=1,
            grid=(),
            in_specs=[WHOLE] * 4,
            out_specs=[WHOLE] * len(out_shape),
            scratch_shapes=[pltpu.SMEM((acc.shape[0] * (8 + n_refs) + 1,), jnp.int32)],
        ),
        input_output_aliases={2: len(out_shape) - 2, 3: len(out_shape) - 1},
        compiler_params=pltpu.CompilerParams(vmem_limit_bytes=40 * 1024 * 1024),
        cost_estimate=pl.CostEstimate(
            flops=8 * pairs * HEAD_DIM, bytes_accessed=8 * acc.size, transcendentals=pairs
        ),
    )(plan, query, acc, stat, source)


def shards(queries, keys, values, epi_dev, epi_frame, epi_block, valid, ref_local, *, n_tm, n_tok):
    inner = HEADS // n_tok
    n_outer = n_tm // inner
    n_ranks = inner * n_tok
    units = n_ranks * STRIDE
    ref_near = inner % SPAN == 0
    n_refs = 0 if ref_near else n_tok
    blocks = n_ranks * FRAMES_DEV
    rooms = [-(-blocks * share // 32) for share in (*range(19, 27), 28)] if n_outer == 2 else []
    flip = inner // 2 if n_outer == 2 and inner % (2 * SPAN) == 0 else 0

    def device(o, spot):
        return o * inner + (spot + flip * o) % inner

    groups = [
        [device(o, i) * n_tok + t for i in range(inner) for t in range(n_tok)]
        for o in range(n_outer)
    ]

    def exchange(x):
        return lax.all_to_all(x, ("tm", "tok"), 0, 0, axis_index_groups=groups, tiled=True)

    def turn(x):
        pairs = [
            (device(o, i), device((o + 1) % n_outer, i)) for o in range(n_outer) for i in range(inner)
        ]
        return lax.ppermute(x, "tm", pairs)

    my_outer = (lax.axis_index("tm") // inner).astype(jnp.int32)
    plan = make_plan(
        epi_dev, epi_frame, epi_block, valid, ref_local, my_outer, inner, n_tok, flip, rooms
    )
    small = pltpu.CompilerParams(vmem_limit_bytes=24 * 1024 * 1024)
    own = pl.pallas_call(
        split_kernel,
        out_shape=jax.ShapeDtypeStruct((n_ranks, STRIDE, BLOCK, 2 * HEAD_DIM), keys.dtype),
        in_specs=[pl.BlockSpec(memory_space=pltpu.HBM)] * 3,
        out_specs=WHOLE,
        scratch_shapes=[pltpu.VMEM(keys.shape, keys.dtype)] * 3 + [pltpu.SemaphoreType.DMA((3,))],
        compiler_params=small,
    )(*[pltpu.with_memory_space_constraint(x, pltpu.HBM) for x in (queries, keys, values)])
    own = exchange(own).reshape(units, BLOCK, 2 * HEAD_DIM)

    def attend(own, arrivals, spot_row, waiting=()):
        query, acc, stat = near(plan, own, inner, n_tok, spot_row, ref_near)
        acc, stat = stage(plan, own, query, acc, stat, 0, n_ranks, spot_row, n_refs, False)
        arrivals, waiting = list(arrivals), list(waiting)
        low = FAR
        while arrivals:
            if waiting:
                held, acc = lax.optimization_barrier((waiting.pop(0), acc))
                arrivals.append(turn(held))
            arrived = arrivals.pop(0)
            *result, acc, stat = stage(
                plan, arrived, query, acc, stat, low, n_ranks, spot_row, n_refs, not arrivals
            )
            low += arrived.shape[0]
        return result[0]

    def listed(room):
        sizes = (room - room * 2 // 5, room * 2 // 5)

        def run(own):
            first, *later = pack(plan, own, sizes)
            return attend(own, [turn(first)], 2, later)

        return run

    def gathered(own):
        arrivals = [turn(own)]
        for _ in range(n_outer - 2):
            arrivals.append(turn(arrivals[-1]))
        return attend(own, arrivals, 4)

    options = [listed(room) for room in rooms] + [gathered]
    attended = exchange(lax.switch(plan[1, 0], options, own))
    return pl.pallas_call(
        merge_kernel,
        out_shape=jax.ShapeDtypeStruct(queries.shape, queries.dtype),
        in_specs=[WHOLE],
        out_specs=WHOLE,
        compiler_params=small,
    )(attended)


def solution(mesh):
    return jax.shard_map(
        functools.partial(shards, n_tm=mesh.shape["tm"], n_tok=mesh.shape["tok"]),
        mesh=mesh,
        in_specs=(P("tm", "tok", None),) * 3 + (P(),) * 5,
        out_specs=P("tm", "tok", None),
        check_vma=False,
    )
```

```python
import functools
import math

import jax
import jax.numpy as jnp
from jax import lax
from jax.experimental import pallas as pl
from jax.experimental.pallas import tpu as pltpu
from jax.sharding import PartitionSpec as P

HEADS = 16
HEAD_DIM = 64
BLOCK = 128
FRAMES_DEV = 2
ENTRIES = 6
SPAN = 4
FAR = 1024
DEAD = 65536
BATCH_BITS = 2
BATCH = 1 << BATCH_BITS

STRIDE = FRAMES_DEV + 1
WHOLE = pl.BlockSpec(memory_space=pltpu.VMEM)


def split_kernel(q_hbm, k_hbm, v_hbm, out_ref, q_ref, k_ref, v_ref, sems):
    copies = [
        pltpu.make_async_copy(source, target, sems.at[index])
        for index, (source, target) in enumerate(
            ((q_hbm, q_ref), (k_hbm, k_ref), (v_hbm, v_ref))
        )
    ]
    for copy in copies:
        copy.start()
    copies[0].wait()
    lanes_of = [slice(rank * HEAD_DIM, (rank + 1) * HEAD_DIM) for rank in range(out_ref.shape[0])]
    for rank, lanes in enumerate(lanes_of):
        out_ref[rank, FRAMES_DEV] = jnp.concatenate(
            [q_ref[frame, :, lanes] for frame in range(FRAMES_DEV)], 1
        )
    for copy in copies[1:]:
        copy.wait()
    for rank, lanes in enumerate(lanes_of):
        for frame in range(FRAMES_DEV):
            out_ref[rank, frame] = jnp.concatenate(
                [k_ref[frame, :, lanes], v_ref[frame, :, lanes]], 1
            )


def merge_kernel(x_ref, out_ref):
    for frame in range(FRAMES_DEV):
        part = slice(frame * HEAD_DIM, (frame + 1) * HEAD_DIM)
        for rank in range(0, x_ref.shape[0], 2):
            out_ref[frame, :, rank * HEAD_DIM : (rank + 2) * HEAD_DIM] = jnp.concatenate(
                [x_ref[rank, :, part], x_ref[rank + 1, :, part]], 1
            )


def plan_kernel(
    me_ref, ref_ref, dev_hbm, place_hbm, block_hbm, valid_hbm, out_ref, entries, sems,
    *, inner, n_tok, flip, rooms,
):
    copies = [
        pltpu.make_async_copy(array, entries.at[index], sems.at[index])
        for index, array in enumerate((dev_hbm, place_hbm, block_hbm, valid_hbm))
    ]
    for copy in copies:
        copy.start()
    for copy in copies:
        copy.wait()
    n_frames = dev_hbm.shape[0]
    units = inner * n_tok * STRIDE
    group_frames = inner * FRAMES_DEV
    n_outer = n_frames // group_frames
    lanes = out_ref.shape[1]
    f32 = jnp.float32
    me = me_ref[0].astype(f32)
    dev = entries[0]
    spot = (dev % inner + flip * (dev // inner)) % inner
    ids = (dev // inner) * units + (spot * n_tok + entries[2]) * STRIDE + entries[1]
    used = entries[3] > 0
    frame_lane = lax.broadcasted_iota(jnp.int32, (n_frames, lanes), 1)
    hit = jnp.zeros((n_frames, lanes), f32)
    for entry in range(ENTRIES):
        here = (ids[:, entry : entry + 1] == frame_lane) & used[:, entry : entry + 1]
        hit = jnp.where(here, 1.0, hit)
    lane = lax.broadcasted_iota(jnp.int32, (1, lanes), 1)
    unit = (lane % units).astype(f32)
    origin = (lane // units).astype(f32)
    crosses = jnp.zeros((1, lanes), f32)
    for group in range(n_outer):
        rows = lax.slice_in_dim(hit, group * group_frames, (group + 1) * group_frames)
        wanted = jnp.sum(rows, axis=0, keepdims=True)
        crosses = jnp.where(origin != group, wanted + crosses, crosses)

    def count(mask, axis):
        return jnp.sum(jnp.where(mask, 1.0, 0.0), axis=axis, keepdims=True)

    steps = jnp.where(origin > me, me - origin + n_outer, me - origin)
    everything = jnp.where(origin == me, unit, FAR + (steps - 1.0) * units + unit)
    sent, spots, chosen = jnp.zeros_like(origin), everything, jnp.full((1, 1), float(len(rooms)), f32)
    if rooms:
        square_row = lax.broadcasted_iota(jnp.int32, (lanes, lanes), 0)
        square_lane = lax.broadcasted_iota(jnp.int32, (lanes, lanes), 1)

        def column(row):
            return jnp.sum(jnp.where(square_row == square_lane, row, 0.0), axis=1, keepdims=True)

        key = jnp.where(crosses > 0, origin, -1.0)
        uses = column(crosses)
        ahead = (uses > crosses) | ((uses == crosses) & (square_row < square_lane))
        slot = count((column(key) == key) & ahead, 0)
        most = jnp.max(jnp.where(crosses > 0, slot + 1.0, 0.0), axis=1, keepdims=True)
        for index in reversed(range(len(rooms))):
            chosen = jnp.where(most <= rooms[index], float(index), chosen)
        mine = column(jnp.where((crosses > 0) & (origin == me), slot, -1.0))
        sent = jnp.sum(
            jnp.where(mine == square_lane.astype(f32), column(unit), 0.0), axis=0, keepdims=True
        )
        spots = jnp.where(origin == me, unit, FAR + slot)

    row_frame = lax.broadcasted_iota(jnp.int32, (n_frames, lanes), 0).astype(f32)
    wide_lane = frame_lane.astype(f32)
    local_row = row_frame - me * group_frames
    turned = local_row + me * (flip * FRAMES_DEV)
    turned = jnp.where(turned >= group_frames, turned - group_frames, turned) * 8
    turned = jnp.where((local_row >= 0) & (local_row < group_frames), turned, -8.0)

    def places(table):
        listed = jnp.zeros((1, lanes), f32)
        for entry in range(ENTRIES):
            mine, live = ids[:, entry : entry + 1], used[:, entry : entry + 1]
            found = jnp.sum(jnp.where(mine == frame_lane, table, 0.0), axis=1, keepdims=True)
            found = jnp.where(live, found, float(DEAD))
            target = turned + entry
            listed += jnp.sum(jnp.where(target == wide_lane, found, 0.0), axis=0, keepdims=True)
        listed = jnp.where(lane % 8 < ENTRIES, listed, float(DEAD))
        refs = jnp.zeros((1, lanes), f32)
        for local in range(max(1, inner // SPAN)):
            scene = me_ref[0] * inner // SPAN + (local * SPAN + flip * me_ref[0]) % inner // SPAN
            ref_frame = scene * (SPAN * FRAMES_DEV) + ref_ref[scene]
            ref_dev = ref_frame // FRAMES_DEV
            ref_spot = (ref_dev % inner + flip * (ref_dev // inner)) % inner
            base = (ref_dev // inner) * units + ref_spot * n_tok * STRIDE
            for block in range(n_tok):
                which = base + block * STRIDE + ref_frame % FRAMES_DEV
                found = jnp.sum(jnp.where(lane == which, table, 0.0), axis=1, keepdims=True)
                refs = jnp.where(lane == local * n_tok + block, found, refs)
        return [listed, refs]

    rows = [sent, chosen + jnp.zeros_like(origin)] + places(spots) + places(everything)
    for index, row in enumerate(rows):
        out_ref[index : index + 1, :] = row.astype(jnp.int32)


def make_plan(epi_dev, epi_frame, epi_block, valid, ref_local, my_outer, inner, n_tok, flip, rooms):
    n_outer = epi_dev.shape[0] // (inner * FRAMES_DEV)
    n_units = n_outer * inner * n_tok * STRIDE
    lanes = -(-n_units // 128) * 128
    smem, anywhere = pl.BlockSpec(memory_space=pltpu.SMEM), pl.BlockSpec(memory_space=pl.ANY)
    return pl.pallas_call(
        functools.partial(plan_kernel, inner=inner, n_tok=n_tok, flip=flip, rooms=rooms),
        out_shape=jax.ShapeDtypeStruct((8, lanes), jnp.int32),
        in_specs=[smem, smem] + [anywhere] * 4,
        out_specs=WHOLE,
        scratch_shapes=[
            pltpu.VMEM((4,) + epi_dev.shape, jnp.int32),
            pltpu.SemaphoreType.DMA((4,)),
        ],
        compiler_params=pltpu.CompilerParams(vmem_limit_bytes=32 * 1024 * 1024),
    )(my_outer.reshape(1), ref_local, epi_dev, epi_frame, epi_block, valid)


def pack_kernel(plan_ref, own_ref, *targets):
    first = 0
    for target in targets:
        for slot in range(target.shape[0]):
            target[slot] = own_ref[plan_ref[0, first + slot]]
        first += target.shape[0]


def pack(plan, own, sizes):
    return pl.pallas_call(
        pack_kernel,
        out_shape=[jax.ShapeDtypeStruct((size,) + own.shape[1:], own.dtype) for size in sizes],
        grid_spec=pltpu.PrefetchScalarGridSpec(
            num_scalar_prefetch=1,
            grid=(),
            in_specs=[WHOLE],
            out_specs=[WHOLE] * len(sizes),
        ),
        compiler_params=pltpu.CompilerParams(vmem_limit_bytes=24 * 1024 * 1024),
        cost_estimate=pl.CostEstimate(
            flops=0, bytes_accessed=4 * sum(sizes) * own[0].size, transcendentals=0
        ),
    )(plan, own)


def part_of(pairs, query):
    scores = jnp.dot(pairs, query, preferred_element_type=jnp.float32)
    top = jnp.max(scores, axis=0, keepdims=True)
    weights = jnp.exp(scores - top)
    total = jnp.sum(weights, axis=0, keepdims=True)
    attended = jnp.dot(
        pairs.T[HEAD_DIM:], weights.astype(jnp.bfloat16), preferred_element_type=jnp.float32
    )
    return attended, top, total


def near_kernel(plan_ref, own_ref, query_ref, acc_ref, stat_ref, *, n_tok, spot_row, ref_near):
    n_local, n_tiles, _, tile = acc_ref.shape
    inner = n_local // FRAMES_DEV

    @pl.loop(0, inner, unroll=math.gcd(2, inner))
    def _(chip):
        spots = [(chip * n_tok + block) * STRIDE for block in range(n_tok)]
        refs = []
        if ref_near:
            scene = chip // SPAN * n_tok
            refs = [own_ref[plan_ref[spot_row + 1, scene + block]] for block in range(n_tok)]
        turned = [own_ref[spot + FRAMES_DEV].T for spot in spots]
        for frame in range(FRAMES_DEV):
            pairs = jnp.concatenate([own_ref[spot + frame] for spot in spots] + refs, 0)
            local = chip * FRAMES_DEV + frame
            for index in range(n_tiles):
                first = index * tile // BLOCK
                query = jnp.concatenate(
                    [
                        block[frame * HEAD_DIM : (frame + 1) * HEAD_DIM]
                        for block in turned[first : first + tile // BLOCK]
                    ],
                    1,
                ) * jnp.asarray(HEAD_DIM**-0.5, own_ref.dtype)
                query = jnp.concatenate([query, jnp.zeros_like(query)], 0)
                query_ref[local, index] = query
                attended, top, total = part_of(pairs, query)
                acc_ref[local, index] = attended
                stat_ref[local, index, 0:1] = top
                stat_ref[local, index, 1:2] = total


def near(plan, own, inner, n_tok, spot_row, ref_near):
    rows = n_tok * BLOCK
    tile = math.gcd(rows, 256)
    n_local = inner * FRAMES_DEV
    pairs = n_local * rows * (1 + ref_near) * rows
    lead = (n_local, rows // tile)
    return pl.pallas_call(
        functools.partial(near_kernel, n_tok=n_tok, spot_row=spot_row, ref_near=ref_near),
        out_shape=(
            jax.ShapeDtypeStruct(lead + (2 * HEAD_DIM, tile), own.dtype),
            jax.ShapeDtypeStruct(lead + (HEAD_DIM, tile), jnp.float32),
            jax.ShapeDtypeStruct(lead + (2, tile), jnp.float32),
        ),
        grid_spec=pltpu.PrefetchScalarGridSpec(
            num_scalar_prefetch=1,
            grid=(),
            in_specs=[WHOLE],
            out_specs=(WHOLE, WHOLE, WHOLE),
        ),
        compiler_params=pltpu.CompilerParams(vmem_limit_bytes=40 * 1024 * 1024),
        cost_estimate=pl.CostEstimate(
            flops=8 * pairs * HEAD_DIM,
            bytes_accessed=16 * n_local * rows * HEAD_DIM,
            transcendentals=pairs,
        ),
    )(plan, own)


def stage_kernel(
    plan_ref, query_ref, acc_in, stat_in, source_ref, *refs, low, high, spot_row, n_refs, final
):
    acc_ref, stat_ref, items = refs[-3:]
    n_local, n_tiles, _, tile = acc_ref.shape

    def add(found, local, code):
        items[found] = (local << 16) + (code - low)
        return found + ((code >= low) & (code < high)).astype(jnp.int32)

    def listed(local, found):
        for entry in range(ENTRIES):
            found = add(found, local, plan_ref[spot_row, local * 8 + entry])
        for block in range(n_refs):
            found = add(found, local, plan_ref[spot_row + 1, block])
        return found

    found = lax.fori_loop(0, n_local, listed, jnp.int32(0), unroll=math.gcd(16, n_local))

    @pl.loop(0, (found + (BATCH - 1)) >> BATCH_BITS)
    def _(step):
        for index in range(n_tiles):
            parts = []
            for turn in range(BATCH):
                here = step * BATCH + turn < found
                word = items[jnp.where(here, step * BATCH + turn, 0)]
                local = word >> 16
                parts.append((here, local, part_of(source_ref[word & (DEAD - 1)], query_ref[local, index])))
            for here, local, (attended, top, total) in parts:
                old_top = stat_ref[local, index, 0:1]
                new_top = jnp.where(here, jnp.maximum(old_top, top), old_top)
                keep = jnp.exp(old_top - new_top)
                add = jnp.where(here, jnp.exp(jnp.minimum(top - new_top, 0.0)), 0.0)
                acc_ref[local, index] = acc_ref[local, index] * keep + attended * add
                stat_ref[local, index, 1:2] = stat_ref[local, index, 1:2] * keep + total * add
                stat_ref[local, index, 0:1] = new_top

    if not final:
        return
    out_ref = refs[0]
    n_tok = n_tiles * tile // BLOCK
    inner = n_local // FRAMES_DEV

    @pl.loop(0, inner, unroll=math.gcd(4, inner))
    def _(chip):
        for index in range(n_tiles):
            parts = []
            for frame in range(FRAMES_DEV):
                local = chip * FRAMES_DEV + frame
                parts.append(acc_ref[local, index] * (1.0 / stat_ref[local, index][1:2]))
            result = jnp.concatenate(parts, 0).astype(out_ref.dtype).T
            for block in range(tile // BLOCK):
                out_ref[chip * n_tok + index * (tile // BLOCK) + block] = result[
                    block * BLOCK : (block + 1) * BLOCK
                ]


def stage(plan, source, query, acc, stat, low, n_ranks, spot_row, n_refs, final):
    out_shape = [jax.ShapeDtypeStruct(x.shape, x.dtype) for x in (acc, stat)]
    if final:
        result = jax.ShapeDtypeStruct((n_ranks, BLOCK, FRAMES_DEV * HEAD_DIM), query.dtype)
        out_shape = [result] + out_shape
    pairs = 2 * acc.size // HEAD_DIM * BLOCK
    return pl.pallas_call(
        functools.partial(
            stage_kernel, low=low, high=low + source.shape[0], spot_row=spot_row,
            n_refs=n_refs, final=final,
        ),
        out_shape=out_shape,
        grid_spec=pltpu.PrefetchScalarGridSpec(
            num_scalar_prefetch=1,
            grid=(),
            in_specs=[WHOLE] * 4,
            out_specs=[WHOLE] * len(out_shape),
            scratch_shapes=[pltpu.SMEM((acc.shape[0] * (8 + n_refs) + 1,), jnp.int32)],
        ),
        input_output_aliases={2: len(out_shape) - 2, 3: len(out_shape) - 1},
        compiler_params=pltpu.CompilerParams(vmem_limit_bytes=40 * 1024 * 1024),
        cost_estimate=pl.CostEstimate(
            flops=8 * pairs * HEAD_DIM, bytes_accessed=8 * acc.size, transcendentals=pairs
        ),
    )(plan, query, acc, stat, source)


def shards(queries, keys, values, epi_dev, epi_frame, epi_block, valid, ref_local, *, n_tm, n_tok):
    inner = HEADS // n_tok
    n_outer = n_tm // inner
    n_ranks = inner * n_tok
    units = n_ranks * STRIDE
    ref_near = inner % SPAN == 0
    n_refs = 0 if ref_near else n_tok
    blocks = n_ranks * FRAMES_DEV
    rooms = [-(-blocks * share // 32) for share in (*range(19, 27), 28)] if n_outer == 2 else []
    flip = inner // 2 if n_outer == 2 and inner % (2 * SPAN) == 0 else 0

    def device(o, spot):
        return o * inner + (spot + flip * o) % inner

    groups = [
        [device(o, i) * n_tok + t for i in range(inner) for t in range(n_tok)]
        for o in range(n_outer)
    ]

    def exchange(x):
        return lax.all_to_all(x, ("tm", "tok"), 0, 0, axis_index_groups=groups, tiled=True)

    def turn(x):
        pairs = [
            (device(o, i), device((o + 1) % n_outer, i)) for o in range(n_outer) for i in range(inner)
        ]
        return lax.ppermute(x, "tm", pairs)

    my_outer = (lax.axis_index("tm") // inner).astype(jnp.int32)
    plan = make_plan(
        epi_dev, epi_frame, epi_block, valid, ref_local, my_outer, inner, n_tok, flip, rooms
    )
    small = pltpu.CompilerParams(vmem_limit_bytes=24 * 1024 * 1024)
    own = pl.pallas_call(
        split_kernel,
        out_shape=jax.ShapeDtypeStruct((n_ranks, STRIDE, BLOCK, 2 * HEAD_DIM), keys.dtype),
        in_specs=[pl.BlockSpec(memory_space=pltpu.HBM)] * 3,
        out_specs=WHOLE,
        scratch_shapes=[pltpu.VMEM(keys.shape, keys.dtype)] * 3 + [pltpu.SemaphoreType.DMA((3,))],
        compiler_params=small,
    )(*[pltpu.with_memory_space_constraint(x, pltpu.HBM) for x in (queries, keys, values)])
    own = exchange(own).reshape(units, BLOCK, 2 * HEAD_DIM)

    def attend(own, arrivals, spot_row, waiting=()):
        query, acc, stat = near(plan, own, inner, n_tok, spot_row, ref_near)
        acc, stat = stage(plan, own, query, acc, stat, 0, n_ranks, spot_row, n_refs, False)
        arrivals, waiting = list(arrivals), list(waiting)
        low = FAR
        while arrivals:
            if waiting:
                held, acc = lax.optimization_barrier((waiting.pop(0), acc))
                arrivals.append(turn(held))
            arrived = arrivals.pop(0)
            *result, acc, stat = stage(
                plan, arrived, query, acc, stat, low, n_ranks, spot_row, n_refs, not arrivals
            )
            low += arrived.shape[0]
        return result[0]

    def listed(room):
        sizes = (room - room * 2 // 5, room * 2 // 5)

        def run(own):
            first, *later = pack(plan, own, sizes)
            return attend(own, [turn(first)], 2, later)

        return run

    def gathered(own):
        arrivals = [turn(own)]
        for _ in range(n_outer - 2):
            arrivals.append(turn(arrivals[-1]))
        return attend(own, arrivals, 4)

    options = [listed(room) for room in rooms] + [gathered]
    attended = exchange(lax.switch(plan[1, 0], options, own))
    return pl.pallas_call(
        merge_kernel,
        out_shape=jax.ShapeDtypeStruct(queries.shape, queries.dtype),
        in_specs=[WHOLE],
        out_specs=WHOLE,
        compiler_params=small,
    )(attended)


def solution(mesh):
    return jax.shard_map(
        functools.partial(shards, n_tm=mesh.shape["tm"], n_tok=mesh.shape["tok"]),
        mesh=mesh,
        in_specs=(P("tm", "tok", None),) * 3 + (P(),) * 5,
        out_specs=P("tm", "tok", None),
        check_vma=False,
    )
```
